256 devices in a mesh: section: 8 (over z_lo, core), dp: 32 (over z_hi, x, y).
Axes of the slice: x: 4, y: 4, z: 8 (z_hi: 2, z_lo: 4; z = z_hi * 4 + z_lo), core: 2. Of those that a mesh axis runs over, the one named last changes fastest.
Arguments:
- inflow: bfloat16 [8, 4096, 7168], P('section', 'dp'), may hold values from -6 to 6
- entering: bfloat16 [1, 4096, 7168], P(None, 'dp'), may hold values from -6 to 6
- arrive_grad: bfloat16 [8, 4096, 7168], P('section', 'dp'), may hold values from -12 to 12
- enter_grad: bfloat16 [1, 4096, 7168], P(None, 'dp'), may hold values from -6 to 6
- stashed: bfloat16 [8, 4096, 7168], P('section', 'dp'), may hold values from -12 to 12
- w_down: bfloat16 [8, 7168, 256], P('section', 'dp'), may hold values from -0.0625 to 0.0625
- w_up: bfloat16 [8, 256, 7168], P('section', None, 'dp'), may hold values from -0.375 to 0.375
- norm_gain: float32 [8, 7168], P('section'), may hold values from 0.25 to 1.75
- latent_gain: float32 [8, 256], P('section'), may hold values from 0.25 to 1.75
Outputs:
- leaving_acts: bfloat16 [8, 4096, 7168], P('section', 'dp')
- leaving_grads: bfloat16 [8, 4096, 7168], P('section', 'dp')
- grad_down: float32 [8, 7168, 256], P('section', 'dp')
- grad_up: float32 [8, 256, 7168], P('section', None, 'dp')
- grad_norm_gain: float32 [8, 7168], P('section', 'dp')
- grad_latent_gain: float32 [8, 256], P('section', 'dp')
The draws below stay inside these ranges and needn't reach their ends.
All inputs are finite; a program needn't handle non-finite values.
Results may differ from the reference program's by a relative error of at most 0.0062.
Values may be sent and summed in bfloat16 or wider, within the bound.
A program may use at most 128 MiB of HBM per device.

```python
import jax
import jax.numpy as jnp
from jax import lax

D = 7168
R = 256
TICKS = 2
SECTIONS = 8
TOKENS = 4096


def spiked(values, rng, source, target, shards_of, factor):
    def block_of(position):
        return (jnp.arange(values.shape[position]) // (values.shape[position] // shards_of)).reshape((-1,) + (1,) * (values.ndim - 1 - position))

    one_side = jax.random.permutation(rng, shards_of)[block_of(target)]
    far = (block_of(target) + shards_of // 2) % shards_of
    return jnp.where((block_of(source) == one_side) | (block_of(source) == far), factor * values, values)


def levels(rng, shape, shards, least, largest):
    gain = 1.0
    for dim, shards_of in shards:
        heights = jax.random.uniform(jax.random.fold_in(jax.random.fold_in(rng, 6), dim), (shards_of,), jnp.float32, least / len(shards), largest / len(shards))
        gain = gain * jnp.repeat(jnp.exp(heights), shape[dim] // shards_of).reshape((-1,) + (1,) * (len(shape) - 1 - dim))
    return gain


def scatter_about(own_key, shape, spread, reach, pieces=(), dtype=jnp.bfloat16):
    array = spread * jax.random.normal(own_key, shape, jnp.float32)
    if pieces:
        array = array * levels(own_key, shape, pieces, -0.22, 0.18)
    return jnp.clip(array, -reach, reach).astype(dtype)


def heavy_noise(stream_key, extent, spread, reach, split, heavy, held_as=jnp.bfloat16):
    entries = spread * jax.random.normal(stream_key, extent, jnp.float32)
    if split:
        entries = entries * levels(stream_key, extent, split, -0.22, 0.18)
    return jnp.clip(spiked(entries, jax.random.fold_in(stream_key, 3), *heavy), -reach, reach).astype(held_as)


def setup_inputs(seed: int = 0) -> dict:
    keys = jax.random.split(jax.random.key(seed), 10)
    return {
        "inflow": scatter_about(keys[0], (SECTIONS, TOKENS, D), 1.0, 6.0, ((0, 8), (1, 32))),
        "entering": scatter_about(keys[1], (TICKS - 1, TOKENS, D), 1.0, 6.0, ((1, 32),)),
        "arrive_grad": heavy_noise(keys[2], (SECTIONS, TOKENS, D), 1.0, 12.0, ((0, 8), (1, 32)), (1, 2, 32, 2.75)),
        "enter_grad": scatter_about(keys[3], (TICKS - 1, TOKENS, D), 1.0, 6.0, ((1, 32),)),
        "stashed": heavy_noise(keys[4], (SECTIONS, TOKENS, D), 1.0, 12.0, ((0, 8), (1, 32)), (1, 2, 32, 2.75)),
        "w_down": scatter_about(keys[5], (SECTIONS, D, R), D ** -0.5, 0.0625, ((0, 8), (1, 32))),
        "w_up": scatter_about(keys[6], (SECTIONS, R, D), R ** -0.5, 0.375, ((0, 8), (2, 32))),
        "norm_gain": jnp.clip(1.0 + 0.15 * jax.random.normal(keys[7], (SECTIONS, D), jnp.float32), 0.25, 1.75),
        "latent_gain": jnp.clip(1.0 + 0.15 * jax.random.normal(keys[8], (SECTIONS, R), jnp.float32), 0.25, 1.75),
    }


epsilon = 1e-06

def forward_block(rows_in, down, upward, gain_in, gain_lat):
    wide_in = rows_in.astype(jnp.float32)
    in_scale = lax.rsqrt(lax.optimization_barrier(jnp.mean(wide_in * wide_in, axis=-1, keepdims=True)) + epsilon)
    normed = (wide_in * in_scale * gain_in).astype(jnp.bfloat16)
    latent = jnp.dot(normed, down, preferred_element_type=jnp.float32)
    lat_scale = lax.rsqrt(lax.optimization_barrier(jnp.mean(latent * latent, axis=-1, keepdims=True)) + epsilon)
    lat_norm = latent * lat_scale
    lat_out = (lat_norm * gain_lat).astype(jnp.bfloat16)
    result = (wide_in + jnp.dot(lat_out, upward, preferred_element_type=jnp.float32)).astype(jnp.bfloat16)
    return (result, (wide_in, in_scale, normed, lat_norm, lat_scale, lat_out))

def backward_block(rows_in, grad_rows, down, upward, gain_in, gain_lat):
    _, saved = forward_block(rows_in, down, upward, gain_in, gain_lat)
    wide_in, in_scale, normed, lat_norm, lat_scale, lat_out = saved
    grad_lat = jnp.dot(grad_rows, upward.T, preferred_element_type=jnp.float32)
    grad_upward = jnp.dot(lat_out.T, grad_rows, preferred_element_type=jnp.float32)
    grad_glat = lax.optimization_barrier(jnp.sum(grad_lat * lat_norm, axis=0))
    grad_norm = grad_lat * gain_lat
    grad_raw = lat_scale * (grad_norm - lat_norm * lax.optimization_barrier(jnp.mean(grad_norm * lat_norm, axis=-1, keepdims=True)))
    grad_half = grad_raw.astype(jnp.bfloat16)
    grad_normed = jnp.dot(grad_half, down.T, preferred_element_type=jnp.float32)
    grad_downward = jnp.dot(normed.T, grad_half, preferred_element_type=jnp.float32)
    in_norm = wide_in * in_scale
    grad_gin = lax.optimization_barrier(jnp.sum(grad_normed * in_norm, axis=0))
    grad_in = grad_normed * gain_in
    grad_back = (grad_rows.astype(jnp.float32) + in_scale * (grad_in - in_norm * lax.optimization_barrier(jnp.mean(grad_in * in_norm, axis=-1, keepdims=True)))).astype(jnp.bfloat16)
    return (grad_back, grad_downward, grad_upward, grad_gin, grad_glat)

def reference(inflow, entering, arrive_grad, enter_grad, stashed, w_down, w_up, norm_gain, latent_gain):
    acts_now = [inflow[section_id] for section_id in range(SECTIONS)]
    grads_now = [arrive_grad[section_id] for section_id in range(SECTIONS)]
    stored = [stashed[section_id] for section_id in range(SECTIONS)]
    sum_down = [jnp.zeros((D, R), jnp.float32) for section_id in range(SECTIONS)]
    sum_up = [jnp.zeros((R, D), jnp.float32) for section_id in range(SECTIONS)]
    sum_gin = [jnp.zeros((D,), jnp.float32) for section_id in range(SECTIONS)]
    sum_glat = [jnp.zeros((R,), jnp.float32) for section_id in range(SECTIONS)]
    for tick_id in range(TICKS):
        results = []
        backs = []
        for section_id in range(SECTIONS):
            result, _ = forward_block(acts_now[section_id], w_down[section_id], w_up[section_id], norm_gain[section_id], latent_gain[section_id])
            results.append(result)
            grad_back, g_down, g_up, g_gin, g_glat = backward_block(stored[section_id], grads_now[section_id], w_down[section_id], w_up[section_id], norm_gain[section_id], latent_gain[section_id])
            backs.append(grad_back)
            sum_down[section_id] = sum_down[section_id] + g_down
            sum_up[section_id] = sum_up[section_id] + g_up
            sum_gin[section_id] = sum_gin[section_id] + g_gin
            sum_glat[section_id] = sum_glat[section_id] + g_glat
        stored = list(acts_now)
        if tick_id < TICKS - 1:
            acts_now = [entering[tick_id]] + results[:-1]
            grads_now = backs[1:] + [enter_grad[tick_id]]
    return (jnp.stack(results), jnp.stack(backs), jnp.stack(sum_down), jnp.stack(sum_up), jnp.stack(sum_gin), jnp.stack(sum_glat))
```

```python
import functools

import jax
import jax.numpy as jnp
from jax import lax
from jax.experimental import pallas as pl
from jax.experimental.pallas import tpu as pltpu
from jax.sharding import PartitionSpec as P

EPS = 1e-06
MESH = pl.DeviceIdType.MESH
F32 = jnp.float32
BF16 = jnp.bfloat16

D = 7168
R = 256
T = 128
UNIT = 224
HALF = 112
NEAR = 64
FAR = HALF - NEAR
ROW = 4 * UNIT
ROWS = D // ROW


def nt(a, b):
    return lax.dot_general(a, b, (((1,), (1,)), ((), ())), preferred_element_type=F32)


def tn(a, b):
    return lax.dot_general(a, b, (((0,), (0,)), ((), ())), preferred_element_type=F32)


def nn(a, b):
    return jnp.dot(a, b, preferred_element_type=F32)


def kernel(
    inflow, entering, arrive, enter, stashed, wd_in, wu_in, gin, glat,
    out_act, out_grad, out_down, out_up, out_lg,
    W, G, X, N, GG, A1, N1, R0, B0, OA, OB,
    land4, land2, landn, landf, land1, landz,
    LAT, LN, LS, LO, GL, RAW, MT, SC, LGP, LGL,
    gsend, grecv, zsend, zrecv, rsend, rrecv, asend, arecv, bsend, brecv,
    lsend, lrecv, isem, osem,
):
    s = lax.axis_index("section")
    d = lax.axis_index("dp")
    zh = d // 16
    x = (d // 4) % 4
    y = d % 4
    other = 1 - zh
    not_last = s < 7
    not_first = s > 0

    def dp_of(zz, xx, yy):
        return zz * 16 + xx * 4 + yy

    def along(axis, k):
        if axis == 0:
            return (s, dp_of(zh, (x + k) % 4, y))
        return (s, dp_of(zh, x, (y + k) % 4))

    partner = (s, dp_of(other, x, y))
    up_dev = (s + 1, d)
    down_dev = (s - 1, d)

    def remote(src, dst, ssem, rsem, dev):
        return pltpu.make_async_remote_copy(
            src_ref=src, dst_ref=dst, send_sem=ssem, recv_sem=rsem, device_id=dev, device_id_type=MESH
        )

    wcopy = [
        pltpu.make_async_copy(ref, W.at[m, zh, x, y], isem.at[m]) for m, ref in enumerate((wd_in, wu_in))
    ]
    for c in wcopy:
        c.start()

    def col(c):
        return pl.ds(pl.multiple_of(c * ROW, 128), ROW)

    def load_start(src, dst_of, sem):
        @pl.loop(0, ROWS)
        def _(c):
            pltpu.make_async_copy(src.at[:, col(c)], dst_of(c), sem).start()

    load_start(stashed, lambda c: X.at[0, c], isem.at[2])
    load_start(inflow, lambda c: X.at[1, c], isem.at[3])
    load_start(arrive, lambda c: GG.at[c, pl.ds(0, T)], isem.at[4])

    barrier = pltpu.get_barrier_semaphore()
    peers = [along(ax, k) for ax in (0, 1) for k in (1, 2, 3)] + [partner]
    peers += [((s + 1) % 8, d), ((s + 7) % 8, d)]
    for dev in peers:
        pl.semaphore_signal(barrier, inc=1, device_id=dev, device_id_type=MESH)
    pl.semaphore_wait(barrier, len(peers))

    @pl.when(s == 0)
    def _():
        @pl.loop(0, ROWS)
        def _(c):
            pltpu.make_async_copy(entering.at[:, col(c)], A1.at[c], arecv.at[c]).start()

    @pl.when(s == 7)
    def _():
        @pl.loop(0, ROWS)
        def _(c):
            pltpu.make_async_copy(enter.at[:, col(c)], GG.at[c, pl.ds(T, T)], brecv.at[c]).start()

    for c in wcopy:
        c.wait()

    def wreg(m, zz, h, i1, i2, r0=0, nr=HALF):
        rows = pl.ds(HALF * h + r0, nr)
        return W.at[m, zz, i2, i1, rows] if h == 0 else W.at[m, zz, i1, i2, rows]

    ALL = pl.ds(0, 4)
    LO2, HI2 = pl.ds(0, 2), pl.ds(2, 2)

    def axes(h):
        return (1, y, 0, x) if h == 0 else (0, x, 1, y)

    def gmsg(m, w, h, i, into=False):
        zz = zh if w == 0 else other
        a1, o1, a2, o2 = axes(h)
        p1, n1 = (o1 + 1) % 4, (o1 + 3) % 4
        p2, n2 = (o2 + 1) % 4, (o2 + 3) % 4
        f1, f2 = (o1 + 2) % 4, (o2 + 2) % 4
        g = functools.partial(wreg, m, zz, h)
        src, land, axis, k = [
            (lambda: g(o1, o2), lambda: g(n1, o2), a1, 1),
            (lambda: g(o1, o2), lambda: g(p1, o2), a1, 3),
            (lambda: g(n1, o2, 0, NEAR), lambda: g(f1, o2, 0, NEAR), a1, 1),
            (lambda: g(p1, o2, NEAR, FAR), lambda: g(f1, o2, NEAR, FAR), a1, 3),
            (lambda: g(ALL, o2), lambda: g(ALL, n2), a2, 1),
            (lambda: g(ALL, o2), lambda: g(ALL, p2), a2, 3),
            (lambda: g(LO2, n2), lambda: g(LO2, f2), a2, 1),
            (lambda: g(HI2, p2), lambda: g(HI2, f2), a2, 3),
        ][i]
        idx = ((m * 2 + w) * 2 + h) * 8 + i
        ref = land() if into else src()
        return remote(ref, ref, gsend.at[idx], grecv.at[idx], along(axis, k))

    def g_send(m, w, i):
        for h in (0, 1):
            gmsg(m, w, h, i).start()

    def g_step(m, w, got, then):
        for h in (0, 1):
            gmsg(m, w, h, got, True).wait_recv()
            if then is not None:
                gmsg(m, w, h, then).start()

    def g1_start(m, w):
        g_send(m, w, 0)
        g_send(m, w, 1)

    def g1_forward(m, w):
        g_step(m, w, 0, 2)
        g_step(m, w, 1, 3)

    def g2_start(m, w):
        g_step(m, w, 2, None)
        g_step(m, w, 3, None)
        g_send(m, w, 4)
        g_send(m, w, 5)

    def g2_forward(m, w):
        g_step(m, w, 4, 6)
        g_step(m, w, 5, 7)

    def g_done(m, w):
        g_step(m, w, 6, None)
        g_step(m, w, 7, None)

    def zcopy(m):
        own = W.at[m, zh, x, y]
        return remote(own, own, zsend.at[m], zrecv.at[m], partner)

    def zwait(m):
        far = W.at[m, other, x, y]
        remote(far, far, zsend.at[m], zrecv.at[m], partner).wait_recv()

    def gain(c):
        return gin[:, col(c)]

    def norms(src_of, scale_of, dst_of):
        def sq(c, acc):
            v = src_of(c)[...].astype(F32)
            return acc + jnp.sum(v * v, axis=-1, keepdims=True)

        total = lax.fori_loop(0, ROWS, sq, jnp.zeros((T, 1), F32))
        scale_of()[...] = lax.rsqrt(total * (1.0 / D) + EPS)

        @pl.loop(0, ROWS)
        def _(c):
            dst_of(c)[...] = (src_of(c)[...].astype(F32) * scale_of()[...] * gain(c)).astype(BF16)

    def wrow(m, zz, xx):
        return W[m, zz, xx].reshape(ROW, R)

    def latent_half(zz, rows_of, acc):
        @pl.loop(0, 4)
        def _(xx):
            acc[...] += nn(rows_of(zz * 4 + xx), wrow(0, zz, xx))

    def grad_lat_half(zz, k):
        @pl.loop(0, 4)
        def _(xx):
            GL[k] += nn(GG[zz * 4 + xx, pl.ds(k * T, T)], wrow(1, zz, xx))

    def raw_grad(k):
        rows = pl.ds(k * T, T)
        gl, ln, ls = GL[k], LN[rows], LS[rows]
        gn = gl * glat[...]
        m = jnp.mean(gn * ln, axis=-1, keepdims=True)
        raw = (ls * (gn - ln * m)).astype(BF16)
        RAW[rows] = raw
        MT[k] = jnp.sum(raw.astype(F32) * LAT[rows], axis=-1, keepdims=True) * (1.0 / D)
        return jnp.sum(gl * ln, axis=0, keepdims=True)

    def back_row(k, zz, xx):
        c = zz * 4 + xx
        grad_in = nt(RAW[pl.ds(k * T, T)], wrow(0, zz, xx)) * gain(c)
        sc = SC[k]
        in_norm = X[k, c].astype(F32) * sc
        g = GG[c, pl.ds(k * T, T)].astype(F32)
        return (g + sc * (grad_in - in_norm * MT[k])).astype(BF16)

    def act_copy(c):
        return remote(R0.at[c], A1.at[c], asend.at[c], arecv.at[c], up_dev)

    def back_copy(c):
        return remote(B0.at[c], GG.at[c, pl.ds(T, T)], bsend.at[c], brecv.at[c], down_dev)

    def result_half(zz):
        @pl.loop(0, 4)
        def _(xx):
            c = zz * 4 + xx
            R0[c] = (X[1, c].astype(F32) + nt(LO[pl.ds(T, T)], wrow(1, zz, xx))).astype(BF16)

            @pl.when(not_last)
            def _():
                act_copy(c).start()

    for m in (0, 1):
        zcopy(m).start()
        g1_start(m, 0)
    LAT[...] = jnp.zeros_like(LAT)
    GL[...] = jnp.zeros_like(GL)
    pltpu.make_async_copy(X.at[0], X.at[0], isem.at[2]).wait()
    norms(lambda c: X.at[0, c], lambda: SC.at[0], lambda c: N.at[c, pl.ds(0, T)])
    g1_forward(0, 0)
    g1_forward(1, 0)
    g2_start(0, 0)
    pltpu.make_async_copy(X.at[1], X.at[1], isem.at[3]).wait()
    norms(lambda c: X.at[1, c], lambda: SC.at[1], lambda c: N.at[c, pl.ds(T, T)])
    g2_start(1, 0)
    for m in (0, 1):
        zwait(m)
        g1_start(m, 1)
    g2_forward(0, 0)
    g1_forward(0, 1)
    g1_forward(1, 1)
    g2_forward(1, 0)
    g2_start(0, 1)
    g_done(0, 0)
    latent_half(zh, lambda c: N[c], LAT)
    g2_start(1, 1)
    g2_forward(0, 1)
    g_done(1, 0)
    first_half = GG.at[:, pl.ds(0, T)]
    pltpu.make_async_copy(first_half, first_half, isem.at[4]).wait()
    grad_lat_half(zh, 0)
    g2_forward(1, 1)
    g_done(0, 1)
    latent_half(other, lambda c: N[c], LAT)
    lat = LAT[...]
    lat_scale = lax.rsqrt(jnp.mean(lat * lat, axis=-1, keepdims=True) + EPS)
    LS[...] = lat_scale
    LN[...] = lat * lat_scale
    LO[...] = (lat * lat_scale * glat[...]).astype(BF16)
    result_half(zh)
    g_done(1, 1)
    grad_lat_half(other, 0)
    lg0 = raw_grad(0)

    def send_back_half(zz):
        @pl.loop(0, 4)
        def _(xx):
            c = zz * 4 + xx
            B0[c] = back_row(0, zz, xx)

            @pl.when(not_first)
            def _():
                back_copy(c).start()

    send_back_half(other)
    send_back_half(zh)
    result_half(other)

    def greg(m, zz, h, i1, i2, r0=0, nr=HALF):
        rows = pl.ds(HALF * h + r0, nr)
        return G.at[m, zz, i1, i2, rows] if h == 0 else G.at[m, zz, i2, i1, rows]

    def raxes(h):
        return (0, x, 1, y) if h == 0 else (1, y, 0, x)

    def rmsg(m, w, h, i):
        zz = other if w == 0 else zh
        a1, o1, a2, o2 = raxes(h)
        p1, n1, f1 = (o1 + 1) % 4, (o1 + 3) % 4, (o1 + 2) % 4
        p2, n2, f2 = (o2 + 1) % 4, (o2 + 3) % 4, (o2 + 2) % 4
        g = functools.partial(greg, m, zz, h)
        q = (m * 2 + w) * 2 + h
        src, land, axis, k = [
            (lambda: g(f1, LO2), land2.at[q, 0], a1, 1),
            (lambda: g(f1, HI2), land2.at[q, 1], a1, 3),
            (lambda: g(p1, ALL), land4.at[q, 0], a1, 1),
            (lambda: g(n1, ALL), land4.at[q, 1], a1, 3),
            (lambda: g(o1, f2, 0, NEAR), landn.at[q], a2, 1),
            (lambda: g(o1, f2, NEAR, FAR), landf.at[q], a2, 3),
            (lambda: g(o1, p2), land1.at[q, 0], a2, 1),
            (lambda: g(o1, n2), land1.at[q, 1], a2, 3),
        ][i]
        return remote(src(), land, rsend.at[q * 8 + i], rrecv.at[q * 8 + i], along(axis, k))

    def add_into(ref, *lands):
        total = ref[...].astype(F32)
        for land in lands:
            total = total + land[...].astype(F32)
        ref[...] = total.astype(BF16)

    def r_ctx(m, w, h):
        zz = other if w == 0 else zh
        _, o1, _, o2 = raxes(h)
        return functools.partial(greg, m, zz, h), o1, o2, (m * 2 + w) * 2 + h

    def r1_start(m, w):
        for h in (0, 1):
            rmsg(m, w, h, 0).start()
            rmsg(m, w, h, 1).start()

    def r1_relay(m, w):
        for h in (0, 1):
            g, o1, o2, q = r_ctx(m, w, h)
            rmsg(m, w, h, 0).wait_recv()
            add_into(g((o1 + 1) % 4, LO2), land2.at[q, 0])
            rmsg(m, w, h, 2).start()
        for h in (0, 1):
            g, o1, o2, q = r_ctx(m, w, h)
            rmsg(m, w, h, 1).wait_recv()
            add_into(g((o1 + 3) % 4, HI2), land2.at[q, 1])
            rmsg(m, w, h, 3).start()

    def r2_start(m, w):
        for h in (0, 1):
            g, o1, o2, q = r_ctx(m, w, h)
            rmsg(m, w, h, 2).wait_recv()
            rmsg(m, w, h, 3).wait_recv()
            add_into(g(o1, ALL), land4.at[q, 0], land4.at[q, 1])
            rmsg(m, w, h, 4).start()
            rmsg(m, w, h, 5).start()

    def r2_relay(m, w):
        for h in (0, 1):
            g, o1, o2, q = r_ctx(m, w, h)
            rmsg(m, w, h, 4).wait_recv()
            add_into(g(o1, (o2 + 1) % 4, 0, NEAR), landn.at[q])
            rmsg(m, w, h, 6).start()
            rmsg(m, w, h, 5).wait_recv()
            add_into(g(o1, (o2 + 3) % 4, NEAR, FAR), landf.at[q])
            rmsg(m, w, h, 7).start()

    def zgrad(m):
        return remote(G.at[m, other, x, y], landz.at[m], zsend.at[2 + m], zrecv.at[2 + m], partner)

    def r_done(m, w):
        for h in (0, 1):
            g, o1, o2, q = r_ctx(m, w, h)
            rmsg(m, w, h, 6).wait_recv()
            rmsg(m, w, h, 7).wait_recv()
            if w == 0:
                add_into(g(o1, o2), land1.at[q, 0], land1.at[q, 1])
        if w == 0:
            zgrad(m).start()
        else:
            zgrad(m).wait_recv()
            out = out_down if m == 0 else out_up
            for h in (0, 1):
                g, o1, o2, q = r_ctx(m, w, h)
                rows = pl.ds(HALF * h, HALF)
                out[rows] = (
                    g(o1, o2)[...].astype(F32)
                    + land1[q, 0].astype(F32)
                    + land1[q, 1].astype(F32)
                    + landz[m, rows].astype(F32)
                )

    def up_half(zz):
        @pl.loop(0, 4)
        def _(xx):
            c = zz * 4 + xx
            back_copy(c).wait_recv()
            G[1, zz, xx] = tn(GG[c], LO[...]).astype(BF16).reshape(4, UNIT, R)
            GL[1] += nn(GG[c, pl.ds(T, T)], wrow(1, zz, xx))

    def down_half(zz):
        @pl.loop(0, 4)
        def _(xx):
            G[0, zz, xx] = tn(N[zz * 4 + xx], RAW[...]).astype(BF16).reshape(4, UNIT, R)

    def out_copy(src, dst, c, sem):
        return pltpu.make_async_copy(src.at[c], dst.at[:, col(c)], sem)

    def out_back_half(zz):
        @pl.loop(0, 4)
        def _(xx):
            c = zz * 4 + xx
            OB[c] = back_row(1, zz, xx)
            out_copy(OB, out_grad, c, osem.at[1]).start()

    def lmsg(i):
        axis, k = ((1, 1), (1, 2), (1, 3), (0, 1), (0, 2), (0, 3), (None, 0))[i]
        dev = partner if axis is None else along(axis, k)
        stage = 0 if i < 3 else 1 if i < 6 else 2
        return remote(LGP.at[stage], LGL.at[i], lsend.at[i], lrecv.at[i], dev)

    def lg_stage(stage):
        ids = ((0, 1, 2), (3, 4, 5), (6,))[stage]
        total = LGP[stage]
        for i in ids:
            lmsg(i).wait_recv()
            total = total + LGL[i]
        if stage == 2:
            out_lg[...] = total
        else:
            LGP[stage + 1] = total
            for i in ((3, 4, 5), (6,))[stage]:
                lmsg(i).start()

    up_half(other)
    r1_start(1, 0)
    up_half(zh)
    r1_start(1, 1)
    r1_relay(1, 0)
    lg = lg0 + raw_grad(1)
    LGP[0] = jnp.broadcast_to(lg, (8, R))
    for i in (0, 1, 2):
        lmsg(i).start()
    down_half(other)
    r1_start(0, 0)
    r1_relay(1, 1)
    r2_start(1, 0)
    down_half(zh)
    r1_start(0, 1)
    r1_relay(0, 0)
    r2_relay(1, 0)
    r2_start(1, 1)
    r1_relay(0, 1)
    r_done(1, 0)
    r2_relay(1, 1)
    r2_start(0, 0)
    lg_stage(0)
    out_back_half(other)
    r2_relay(0, 0)
    lg_stage(1)
    out_back_half(zh)
    r2_start(0, 1)
    r_done(0, 0)
    r_done(1, 1)
    lg_stage(2)

    @pl.loop(0, ROWS)
    def _(c):
        act_copy(c).wait_recv()

    norms(lambda c: A1.at[c], lambda: SC.at[0], lambda c: N1.at[c])
    r2_relay(0, 1)
    GL[0] = jnp.zeros((T, R), F32)
    latent_half(zh, lambda c: N1[c], GL.at[0])
    latent_half(other, lambda c: N1[c], GL.at[0])
    lat1 = GL[0]
    LO[pl.ds(0, T)] = (
        lat1 * lax.rsqrt(jnp.mean(lat1 * lat1, axis=-1, keepdims=True) + EPS) * glat[...]
    ).astype(BF16)

    @pl.loop(0, ROWS)
    def _(c):
        OA[c] = (A1[c].astype(F32) + nt(LO[pl.ds(0, T)], wrow(1, c // 4, c % 4))).astype(BF16)
        out_copy(OA, out_act, c, osem.at[0]).start()

    r_done(0, 1)

    for m in (0, 1):
        zcopy(m).wait_send()
        zgrad(m).wait_send()
        for w in (0, 1):
            for h in (0, 1):
                for i in range(8):
                    gmsg(m, w, h, i).wait_send()
                    rmsg(m, w, h, i).wait_send()
    for i in range(7):
        lmsg(i).wait_send()

    @pl.when(not_last)
    def _():
        @pl.loop(0, ROWS)
        def _(c):
            act_copy(c).wait_send()

    @pl.when(not_first)
    def _():
        @pl.loop(0, ROWS)
        def _(c):
            back_copy(c).wait_send()

    pltpu.make_async_copy(OA, OA, osem.at[0]).wait()
    pltpu.make_async_copy(OB, OB, osem.at[1]).wait()


def on_device(
    inflow, entering, arrive_grad, enter_grad, stashed, w_down, w_up, norm_gain, latent_gain
):
    d = lax.axis_index("dp")
    anyspace = pl.BlockSpec(memory_space=pl.ANY)
    vmem = pl.BlockSpec(memory_space=pltpu.VMEM)
    rows = (ROWS, T, ROW)
    dma = pltpu.SemaphoreType.DMA
    acts, grads, down, up, lg = pl.pallas_call(
        kernel,
        out_shape=(
            jax.ShapeDtypeStruct((T, D), BF16),
            jax.ShapeDtypeStruct((T, D), BF16),
            jax.ShapeDtypeStruct((UNIT, R), F32),
            jax.ShapeDtypeStruct((UNIT, R), F32),
            jax.ShapeDtypeStruct((8, R), F32),
        ),
        in_specs=[anyspace] * 7 + [vmem] * 2,
        out_specs=(anyspace, anyspace, vmem, vmem, vmem),
        scratch_shapes=[
            pltpu.VMEM((2, 2, 4, 4, UNIT, R), BF16),
            pltpu.VMEM((2, 2, 4, 4, UNIT, R), BF16),
            pltpu.VMEM((2,) + rows, BF16),
            pltpu.VMEM((ROWS, 2 * T, ROW), BF16),
            pltpu.VMEM((ROWS, 2 * T, ROW), BF16),
            pltpu.VMEM(rows, BF16),
            pltpu.VMEM(rows, BF16),
            pltpu.VMEM(rows, BF16),
            pltpu.VMEM(rows, BF16),
            pltpu.VMEM(rows, BF16),
            pltpu.VMEM(rows, BF16),
            pltpu.VMEM((8, 2, 4, HALF, R), BF16),
            pltpu.VMEM((8, 2, 2, HALF, R), BF16),
            pltpu.VMEM((8, NEAR, R), BF16),
            pltpu.VMEM((8, FAR, R), BF16),
            pltpu.VMEM((8, 2, HALF, R), BF16),
            pltpu.VMEM((2, UNIT, R), BF16),
            pltpu.VMEM((2 * T, R), F32),
            pltpu.VMEM((2 * T, R), F32),
            pltpu.VMEM((2 * T, 1), F32),
            pltpu.VMEM((2 * T, R), BF16),
            pltpu.VMEM((2, T, R), F32),
            pltpu.VMEM((2 * T, R), BF16),
            pltpu.VMEM((2, T, 1), F32),
            pltpu.VMEM((2, T, 1), F32),
            pltpu.VMEM((3, 8, R), F32),
            pltpu.VMEM((7, 8, R), F32),
            dma((64,)), dma((64,)),
            dma((4,)), dma((4,)),
            dma((64,)), dma((64,)),
            dma((ROWS,)), dma((ROWS,)),
            dma((ROWS,)), dma((ROWS,)),
            dma((7,)), dma((7,)),
            dma((5,)), dma((2,)),
        ],
        compiler_params=pltpu.CompilerParams(
            collective_id=0, has_side_effects=True, vmem_limit_bytes=60 * 1024 * 1024
        ),
        name="relay",
    )(
        inflow[0], entering[0], arrive_grad[0], enter_grad[0], stashed[0],
        w_down[0], w_up[0].T, norm_gain, latent_gain,
    )
    own_gain = lax.dynamic_slice(norm_gain, (0, d * UNIT), (1, UNIT))
    gin = jnp.sum(w_down[0].astype(F32) * down, axis=-1)[None] / own_gain
    glat = lax.dynamic_slice(lg, (0, d * 8), (1, 8))
    return acts[None], grads[None], down[None], up.T[None], gin, glat


def solution(mesh):
    in_specs = (
        P("section", "dp", None),
        P(None, "dp", None),
        P("section", "dp", None),
        P(None, "dp", None),
        P("section", "dp", None),
        P("section", "dp", None),
        P("section", None, "dp"),
        P("section", None),
        P("section", None),
    )
    out_specs = (
        P("section", "dp", None),
        P("section", "dp", None),
        P("section", "dp", None),
        P("section", None, "dp"),
        P("section", "dp"),
        P("section", "dp"),
    )
    return jax.shard_map(
        on_device, mesh=mesh, in_specs=in_specs, out_specs=out_specs, check_vma=False
    )
```

```python
import functools

import jax
import jax.numpy as jnp
from jax import lax
from jax.experimental import pallas as pl
from jax.experimental.pallas import tpu as pltpu
from jax.sharding import PartitionSpec as P

EPS = 1e-06
MESH = pl.DeviceIdType.MESH
F32 = jnp.float32
BF16 = jnp.bfloat16

D = 7168
R = 256
T = 128
UNIT = 224
HALF = 112
NEAR = 64
FAR = HALF - NEAR
ROW = 4 * UNIT
ROWS = D // ROW


def nt(a, b):
    return lax.dot_general(a, b, (((1,), (1,)), ((), ())), preferred_element_type=F32)


def tn(a, b):
    return lax.dot_general(a, b, (((0,), (0,)), ((), ())), preferred_element_type=F32)


def nn(a, b):
    return jnp.dot(a, b, preferred_element_type=F32)


def kernel(
    inflow, entering, arrive, enter, stashed, wd_in, wu_in, gin, glat,
    out_act, out_grad, out_down, out_up, out_lg,
    W, G, X, N, GG, A1, N1, R0, B0, OA, OB,
    land4, land2, landn, landf, land1, landz,
    LAT, LN, LS, LO, GL, RAW, MT, SC, LGP, LGL,
    gsend, grecv, zsend, zrecv, rsend, rrecv, asend, arecv, bsend, brecv,
    lsend, lrecv, isem, osem, go,
):
    s = lax.axis_index("section")
    d = lax.axis_index("dp")
    zh = d // 16
    x = (d // 4) % 4
    y = d % 4
    other = 1 - zh
    core = s % 2
    not_last = s < 7
    not_first = s > 0

    def dp_of(zz, xx, yy):
        return zz * 16 + xx * 4 + yy

    def along(axis, k):
        if axis == 0:
            return (s, dp_of(zh, (x + k) % 4, y))
        return (s, dp_of(zh, x, (y + k) % 4))

    partner = (s, dp_of(other, x, y))
    up_dev = (s + 1, d)
    down_dev = (s - 1, d)

    def remote(src, dst, ssem, rsem, dev):
        return pltpu.make_async_remote_copy(
            src_ref=src, dst_ref=dst, send_sem=ssem, recv_sem=rsem, device_id=dev, device_id_type=MESH
        )

    wcopy = [
        pltpu.make_async_copy(ref, W.at[m, zh, x, y], isem.at[m]) for m, ref in enumerate((wd_in, wu_in))
    ]
    for c in wcopy:
        c.start()

    def col(c):
        return pl.ds(pl.multiple_of(c * ROW, 128), ROW)

    def load_start(src, dst_of, sem):
        @pl.loop(0, ROWS)
        def _(c):
            pltpu.make_async_copy(src.at[:, col(c)], dst_of(c), sem).start()

    load_start(stashed, lambda c: X.at[0, c], isem.at[2])
    load_start(inflow, lambda c: X.at[1, c], isem.at[3])
    load_start(arrive, lambda c: GG.at[c, pl.ds(0, T)], isem.at[4])

    barrier = pltpu.get_barrier_semaphore()
    peers = [along(ax, k) for ax in (0, 1) for k in (1, 2, 3)] + [partner]
    peers += [((s + 1) % 8, d), ((s + 7) % 8, d)]
    for dev in peers:
        pl.semaphore_signal(barrier, inc=1, device_id=dev, device_id_type=MESH)
    pl.semaphore_wait(barrier, len(peers))

    @pl.when(s == 0)
    def _():
        @pl.loop(0, ROWS)
        def _(c):
            pltpu.make_async_copy(entering.at[:, col(c)], A1.at[c], arecv.at[c]).start()

    @pl.when(s == 7)
    def _():
        @pl.loop(0, ROWS)
        def _(c):
            pltpu.make_async_copy(enter.at[:, col(c)], GG.at[c, pl.ds(T, T)], brecv.at[c]).start()

    for c in wcopy:
        c.wait()

    def wreg(m, zz, h, i1, i2, r0=0, nr=HALF):
        rows = pl.ds(HALF * h + r0, nr)
        return W.at[m, zz, i2, i1, rows] if h == 0 else W.at[m, zz, i1, i2, rows]

    ALL = pl.ds(0, 4)
    LO2, HI2 = pl.ds(0, 2), pl.ds(2, 2)

    def axes(h):
        return (1, y, 0, x) if h == 0 else (0, x, 1, y)

    def gmsg(m, w, h, i, into=False):
        zz = zh if w == 0 else other
        a1, o1, a2, o2 = axes(h)
        p1, n1 = (o1 + 1) % 4, (o1 + 3) % 4
        p2, n2 = (o2 + 1) % 4, (o2 + 3) % 4
        f1, f2 = (o1 + 2) % 4, (o2 + 2) % 4
        g = functools.partial(wreg, m, zz, h)
        src, land, axis, k = [
            (lambda: g(o1, o2), lambda: g(n1, o2), a1, 1),
            (lambda: g(o1, o2), lambda: g(p1, o2), a1, 3),
            (lambda: g(n1, o2, 0, NEAR), lambda: g(f1, o2, 0, NEAR), a1, 1),
            (lambda: g(p1, o2, NEAR, FAR), lambda: g(f1, o2, NEAR, FAR), a1, 3),
            (lambda: g(ALL, o2), lambda: g(ALL, n2), a2, 1),
            (lambda: g(ALL, o2), lambda: g(ALL, p2), a2, 3),
            (lambda: g(LO2, n2), lambda: g(LO2, f2), a2, 1),
            (lambda: g(HI2, p2), lambda: g(HI2, f2), a2, 3),
        ][i]
        idx = ((m * 2 + w) * 2 + h) * 8 + i
        ref = land() if into else src()
        return remote(ref, ref, gsend.at[idx], grecv.at[idx], along(axis, k))

    def g_send(m, w, i):
        for h in (0, 1):
            gmsg(m, w, h, i).start()

    def g_step(m, w, got, then):
        for h in (0, 1):
            gmsg(m, w, h, got, True).wait_recv()
            if then is not None:
                gmsg(m, w, h, then).start()

    def g1_start(m, w):
        g_send(m, w, 0)
        g_send(m, w, 1)

    def g1_forward(m, w):
        g_step(m, w, 0, 2)
        g_step(m, w, 1, 3)

    def g2_start(m, w):
        g_step(m, w, 2, None)
        g_step(m, w, 3, None)
        g_send(m, w, 4)
        g_send(m, w, 5)

    def g2_forward(m, w):
        g_step(m, w, 4, 6)
        g_step(m, w, 5, 7)

    def g_done(m, w):
        g_step(m, w, 6, None)
        g_step(m, w, 7, None)

    def zcopy(m):
        own = W.at[m, zh, x, y]
        return remote(own, own, zsend.at[m], zrecv.at[m], partner)

    def zwait(m):
        far = W.at[m, other, x, y]
        remote(far, far, zsend.at[m], zrecv.at[m], partner).wait_recv()

    def gain(c):
        return gin[:, col(c)]

    def norms(src_of, scale_of, dst_of):
        def sq(c, acc):
            v = src_of(c)[...].astype(F32)
            return acc + jnp.sum(v * v, axis=-1, keepdims=True)

        total = lax.fori_loop(0, ROWS, sq, jnp.zeros((T, 1), F32))
        scale_of()[...] = lax.rsqrt(total * (1.0 / D) + EPS)

        @pl.loop(0, ROWS)
        def _(c):
            dst_of(c)[...] = (src_of(c)[...].astype(F32) * scale_of()[...] * gain(c)).astype(BF16)

    def wrow(m, zz, xx):
        return W[m, zz, xx].reshape(ROW, R)

    def latent_half(zz, rows_of, acc):
        @pl.loop(0, 4)
        def _(xx):
            acc[...] += nn(rows_of(zz * 4 + xx), wrow(0, zz, xx))

    def grad_lat_half(zz, k):
        @pl.loop(0, 4)
        def _(xx):
            GL[k] += nn(GG[zz * 4 + xx, pl.ds(k * T, T)], wrow(1, zz, xx))

    def raw_grad(k):
        rows = pl.ds(k * T, T)
        gl, ln, ls = GL[k], LN[rows], LS[rows]
        gn = gl * glat[...]
        m = jnp.mean(gn * ln, axis=-1, keepdims=True)
        raw = (ls * (gn - ln * m)).astype(BF16)
        RAW[rows] = raw
        MT[k] = jnp.sum(raw.astype(F32) * LAT[rows], axis=-1, keepdims=True) * (1.0 / D)
        LGP[0] += jnp.broadcast_to(jnp.sum(gl * ln, axis=0, keepdims=True), (8, R))

    def back_row(k, zz, xx):
        c = zz * 4 + xx
        grad_in = nt(RAW[pl.ds(k * T, T)], wrow(0, zz, xx)) * gain(c)
        sc = SC[k]
        in_norm = X[k, c].astype(F32) * sc
        g = GG[c, pl.ds(k * T, T)].astype(F32)
        return (g + sc * (grad_in - in_norm * MT[k])).astype(BF16)

    def act_copy(c):
        return remote(R0.at[c], A1.at[c], asend.at[c], arecv.at[c], up_dev)

    def back_copy(c):
        return remote(B0.at[c], GG.at[c, pl.ds(T, T)], bsend.at[c], brecv.at[c], down_dev)

    def result_half(zz):
        @pl.loop(0, 4)
        def _(xx):
            c = zz * 4 + xx
            R0[c] = (X[1, c].astype(F32) + nt(LO[pl.ds(T, T)], wrow(1, zz, xx))).astype(BF16)

            @pl.when(not_last)
            def _():
                act_copy(c).start()

    def send_back_half(zz):
        @pl.loop(0, 4)
        def _(xx):
            c = zz * 4 + xx
            B0[c] = back_row(0, zz, xx)

            @pl.when(not_first)
            def _():
                back_copy(c).start()

    def greg(m, zz, h, i1, i2, r0=0, nr=HALF):
        rows = pl.ds(HALF * h + r0, nr)
        return G.at[m, zz, i1, i2, rows] if h == 0 else G.at[m, zz, i2, i1, rows]

    def raxes(h):
        return (0, x, 1, y) if h == 0 else (1, y, 0, x)

    def rmsg(m, w, h, i):
        zz = other if w == 0 else zh
        a1, o1, a2, o2 = raxes(h)
        p1, n1, f1 = (o1 + 1) % 4, (o1 + 3) % 4, (o1 + 2) % 4
        p2, n2, f2 = (o2 + 1) % 4, (o2 + 3) % 4, (o2 + 2) % 4
        g = functools.partial(greg, m, zz, h)
        q = (m * 2 + w) * 2 + h
        src, land, axis, k = [
            (lambda: g(f1, LO2), land2.at[q, 0], a1, 1),
            (lambda: g(f1, HI2), land2.at[q, 1], a1, 3),
            (lambda: g(p1, ALL), land4.at[q, 0], a1, 1),
            (lambda: g(n1, ALL), land4.at[q, 1], a1, 3),
            (lambda: g(o1, f2, 0, NEAR), landn.at[q], a2, 1),
            (lambda: g(o1, f2, NEAR, FAR), landf.at[q], a2, 3),
            (lambda: g(o1, p2), land1.at[q, 0], a2, 1),
            (lambda: g(o1, n2), land1.at[q, 1], a2, 3),
        ][i]
        return remote(src(), land, rsend.at[q * 8 + i], rrecv.at[q * 8 + i], along(axis, k))

    def add_into(ref, *lands):
        total = ref[...].astype(F32)
        for land in lands:
            total = total + land[...].astype(F32)
        ref[...] = total.astype(BF16)

    def r_ctx(m, w, h):
        zz = other if w == 0 else zh
        _, o1, _, o2 = raxes(h)
        return functools.partial(greg, m, zz, h), o1, o2, (m * 2 + w) * 2 + h

    def r1_start(m, w):
        for h in (0, 1):
            rmsg(m, w, h, 0).start()
            rmsg(m, w, h, 1).start()

    def r1_relay(m, w):
        for h in (0, 1):
            g, o1, o2, q = r_ctx(m, w, h)
            rmsg(m, w, h, 0).wait_recv()
            add_into(g((o1 + 1) % 4, LO2), land2.at[q, 0])
            rmsg(m, w, h, 2).start()
        for h in (0, 1):
            g, o1, o2, q = r_ctx(m, w, h)
            rmsg(m, w, h, 1).wait_recv()
            add_into(g((o1 + 3) % 4, HI2), land2.at[q, 1])
            rmsg(m, w, h, 3).start()

    def r2_start(m, w):
        for h in (0, 1):
            g, o1, o2, q = r_ctx(m, w, h)
            rmsg(m, w, h, 2).wait_recv()
            rmsg(m, w, h, 3).wait_recv()
            add_into(g(o1, ALL), land4.at[q, 0], land4.at[q, 1])
            rmsg(m, w, h, 4).start()
            rmsg(m, w, h, 5).start()

    def r2_relay(m, w):
        for h in (0, 1):
            g, o1, o2, q = r_ctx(m, w, h)
            rmsg(m, w, h, 4).wait_recv()
            add_into(g(o1, (o2 + 1) % 4, 0, NEAR), landn.at[q])
            rmsg(m, w, h, 6).start()
            rmsg(m, w, h, 5).wait_recv()
            add_into(g(o1, (o2 + 3) % 4, NEAR, FAR), landf.at[q])
            rmsg(m, w, h, 7).start()

    def zgrad(m):
        return remote(G.at[m, other, x, y], landz.at[m], zsend.at[2 + m], zrecv.at[2 + m], partner)

    def r_done(m, w):
        for h in (0, 1):
            g, o1, o2, q = r_ctx(m, w, h)
            rmsg(m, w, h, 6).wait_recv()
            rmsg(m, w, h, 7).wait_recv()
            if w == 0:
                add_into(g(o1, o2), land1.at[q, 0], land1.at[q, 1])
        if w == 0:
            zgrad(m).start()
        else:
            zgrad(m).wait_recv()
            out = out_down if m == 0 else out_up
            for h in (0, 1):
                g, o1, o2, q = r_ctx(m, w, h)
                rows = pl.ds(HALF * h, HALF)
                out[rows] = (
                    g(o1, o2)[...].astype(F32)
                    + land1[q, 0].astype(F32)
                    + land1[q, 1].astype(F32)
                    + landz[m, rows].astype(F32)
                )

    def up_half(zz):
        @pl.loop(0, 4)
        def _(xx):
            c = zz * 4 + xx
            back_copy(c).wait_recv()
            G[1, zz, xx] = tn(GG[c], LO[...]).astype(BF16).reshape(4, UNIT, R)

    def down_half(zz):
        @pl.loop(0, 4)
        def _(xx):
            G[0, zz, xx] = tn(N[zz * 4 + xx], RAW[...]).astype(BF16).reshape(4, UNIT, R)

    def out_copy(src, dst, c, sem):
        return pltpu.make_async_copy(src.at[c], dst.at[:, col(c)], sem)

    def out_back_half(zz):
        @pl.loop(0, 4)
        def _(xx):
            c = zz * 4 + xx
            OB[c] = back_row(1, zz, xx)
            out_copy(OB, out_grad, c, osem.at[1]).start()

    def lmsg(i):
        axis, k = ((1, 1), (1, 2), (1, 3), (0, 1), (0, 2), (0, 3), (None, 0))[i]
        dev = partner if axis is None else along(axis, k)
        stage = 0 if i < 3 else 1 if i < 6 else 2
        return remote(LGP.at[stage], LGL.at[i], lsend.at[i], lrecv.at[i], dev)

    def lg_start():
        for i in (0, 1, 2):
            lmsg(i).start()

    def lg_stage(stage):
        ids = ((0, 1, 2), (3, 4, 5), (6,))[stage]
        total = LGP[stage]
        for i in ids:
            lmsg(i).wait_recv()
            total = total + LGL[i]
        if stage == 2:
            out_lg[...] = total
        else:
            LGP[stage + 1] = total
            for i in ((3, 4, 5), (6,))[stage]:
                lmsg(i).start()

    def forward_next():
        @pl.loop(0, ROWS)
        def _(c):
            act_copy(c).wait_recv()

        norms(lambda c: A1.at[c], lambda: SC.at[0], lambda c: N1.at[c])
        GL[0] = jnp.zeros((T, R), F32)
        latent_half(zh, lambda c: N1[c], GL.at[0])
        latent_half(other, lambda c: N1[c], GL.at[0])
        lat1 = GL[0]
        LO[pl.ds(0, T)] = (
            lat1 * lax.rsqrt(jnp.mean(lat1 * lat1, axis=-1, keepdims=True) + EPS) * glat[...]
        ).astype(BF16)

        @pl.loop(0, ROWS)
        def _(c):
            OA[c] = (A1[c].astype(F32) + nt(LO[pl.ds(0, T)], wrow(1, c // 4, c % 4))).astype(BF16)
            out_copy(OA, out_act, c, osem.at[0]).start()

    LAT[...] = jnp.zeros_like(LAT)
    GL[...] = jnp.zeros_like(GL)
    LGP[0] = jnp.zeros((8, R), F32)
    for m in (0, 1):
        zcopy(m).start()

    @pl.when(core == 0)
    def _():
        g1_start(0, 0)
        g1_start(1, 0)

    pltpu.make_async_copy(X.at[0], X.at[0], isem.at[2]).wait()
    norms(lambda c: X.at[0, c], lambda: SC.at[0], lambda c: N.at[c, pl.ds(0, T)])

    @pl.when(core == 0)
    def _():
        g1_forward(0, 0)
        g1_forward(1, 0)
        g2_start(0, 0)
        g2_start(1, 0)

    pltpu.make_async_copy(X.at[1], X.at[1], isem.at[3]).wait()
    norms(lambda c: X.at[1, c], lambda: SC.at[1], lambda c: N.at[c, pl.ds(T, T)])
    first_half = GG.at[:, pl.ds(0, T)]
    pltpu.make_async_copy(first_half, first_half, isem.at[4]).wait()

    @pl.when(core == 1)
    def _():
        pl.semaphore_wait(go, 1)
        g1_start(0, 0)
        g1_start(1, 0)
        g1_forward(0, 0)
        g1_forward(1, 0)
        g2_start(0, 0)
        g2_start(1, 0)

    for m in (0, 1):
        zwait(m)
        g1_start(m, 1)
    g2_forward(0, 0)
    g1_forward(0, 1)
    g1_forward(1, 1)
    g2_forward(1, 0)
    g2_start(0, 1)
    g2_start(1, 1)

    @pl.when(core == 0)
    def _():
        pl.semaphore_signal(go, inc=1, device_id=up_dev, device_id_type=MESH)

    g_done(0, 0)
    latent_half(zh, lambda c: N[c], LAT)
    g2_forward(0, 1)
    g_done(1, 0)
    grad_lat_half(zh, 0)
    g2_forward(1, 1)
    g_done(0, 1)
    latent_half(other, lambda c: N[c], LAT)
    lat = LAT[...]
    lat_scale = lax.rsqrt(jnp.mean(lat * lat, axis=-1, keepdims=True) + EPS)
    LS[...] = lat_scale
    LN[...] = lat * lat_scale
    LO[...] = (lat * lat_scale * glat[...]).astype(BF16)
    result_half(zh)

    @pl.when(core == 0)
    def _():
        g_done(1, 1)
        grad_lat_half(other, 0)
        raw_grad(0)
        send_back_half(other)
        send_back_half(zh)
        result_half(other)
        up_half(other)
        r1_start(1, 0)
        up_half(zh)
        r1_start(1, 1)
        r1_relay(1, 0)
        grad_lat_half(other, 1)
        grad_lat_half(zh, 1)
        raw_grad(1)
        lg_start()
        down_half(other)
        r1_start(0, 0)
        r1_relay(1, 1)
        r2_start(1, 0)
        down_half(zh)
        r1_start(0, 1)
        r1_relay(0, 0)
        r2_relay(1, 0)
        r2_start(1, 1)
        r1_relay(0, 1)
        r_done(1, 0)
        r2_relay(1, 1)
        r2_start(0, 0)
        lg_stage(0)
        out_back_half(other)
        r2_relay(0, 0)
        lg_stage(1)
        out_back_half(zh)
        r2_start(0, 1)
        r_done(0, 0)
        r_done(1, 1)
        lg_stage(2)
        r2_relay(0, 1)
        forward_next()
        r_done(0, 1)

    @pl.when(core == 1)
    def _():
        up_half(other)
        r1_start(1, 0)
        g_done(1, 1)
        grad_lat_half(other, 0)
        raw_grad(0)
        r1_relay(1, 0)
        send_back_half(other)
        up_half(zh)
        r1_start(1, 1)
        r2_start(1, 0)
        send_back_half(zh)
        r1_relay(1, 1)
        grad_lat_half(other, 1)
        grad_lat_half(zh, 1)
        raw_grad(1)
        lg_start()
        down_half(other)
        r1_start(0, 0)
        r2_relay(1, 0)
        r2_start(1, 1)
        r1_relay(0, 0)
        result_half(other)
        down_half(zh)
        r1_start(0, 1)
        r_done(1, 0)
        r2_relay(1, 1)
        r2_start(0, 0)
        r1_relay(0, 1)
        lg_stage(0)
        out_back_half(other)
        r2_relay(0, 0)
        r_done(1, 1)
        lg_stage(1)
        r2_start(0, 1)
        out_back_half(zh)
        r_done(0, 0)
        lg_stage(2)
        r2_relay(0, 1)
        forward_next()
        r_done(0, 1)

    for m in (0, 1):
        zcopy(m).wait_send()
        zgrad(m).wait_send()
        for w in (0, 1):
            for h in (0, 1):
                for i in range(8):
                    gmsg(m, w, h, i).wait_send()
                    rmsg(m, w, h, i).wait_send()
    for i in range(7):
        lmsg(i).wait_send()

    @pl.when(not_last)
    def _():
        @pl.loop(0, ROWS)
        def _(c):
            act_copy(c).wait_send()

    @pl.when(not_first)
    def _():
        @pl.loop(0, ROWS)
        def _(c):
            back_copy(c).wait_send()

    pltpu.make_async_copy(OA, OA, osem.at[0]).wait()
    pltpu.make_async_copy(OB, OB, osem.at[1]).wait()


def finish(acts, grads, down, up, lg, wd, gain, o_acts, o_grads, o_down, o_up, o_gin, o_glat, sem, pad):
    d = lax.axis_index("dp")
    for i, (src, dst) in enumerate(((acts, o_acts), (grads, o_grads))):
        for j in range(8):
            rows = pl.ds(16 * j, 16)
            pltpu.make_async_copy(src.at[rows], dst.at[rows], sem.at[i]).start()
    o_down[...] = down[...]
    o_up[...] = up[...]
    pad[pl.ds(0, UNIT)] = down[...] * wd[...].astype(F32)
    pad[pl.ds(UNIT, R - UNIT)] = jnp.zeros((R - UNIT, R), F32)
    sums = jnp.sum(pad[...].T, axis=0, keepdims=True)
    first = d * UNIT
    start = pl.multiple_of(jnp.minimum(first // 128 * 128, D - 384), 128)
    window = jnp.broadcast_to(gain[:, pl.ds(start, 384)], (8, 384))
    own = pltpu.roll(window, (384 - (first - start)) % 384, 1)
    o_gin[...] = sums[:, :UNIT] / own[0:1, :UNIT]
    o_glat[...] = pltpu.roll(lg[...], (R - 8 * d) % R, 1)[0:1, :8]
    pltpu.make_async_copy(acts, o_acts, sem.at[0]).wait()
    pltpu.make_async_copy(grads, o_grads, sem.at[1]).wait()


def on_device(
    inflow, entering, arrive_grad, enter_grad, stashed, w_down, w_up, norm_gain, latent_gain
):
    anyspace = pl.BlockSpec(memory_space=pl.ANY)
    vmem = pl.BlockSpec(memory_space=pltpu.VMEM)
    rows = (ROWS, T, ROW)
    dma = pltpu.SemaphoreType.DMA
    acts, grads, down, up, lg = pl.pallas_call(
        kernel,
        out_shape=(
            jax.ShapeDtypeStruct((T, D), BF16),
            jax.ShapeDtypeStruct((T, D), BF16),
            jax.ShapeDtypeStruct((UNIT, R), F32),
            jax.ShapeDtypeStruct((UNIT, R), F32),
            jax.ShapeDtypeStruct((8, R), F32),
        ),
        in_specs=[anyspace] * 7 + [vmem] * 2,
        out_specs=(anyspace, anyspace, vmem, vmem, vmem),
        scratch_shapes=[
            pltpu.VMEM((2, 2, 4, 4, UNIT, R), BF16),
            pltpu.VMEM((2, 2, 4, 4, UNIT, R), BF16),
            pltpu.VMEM((2,) + rows, BF16),
            pltpu.VMEM((ROWS, 2 * T, ROW), BF16),
            pltpu.VMEM((ROWS, 2 * T, ROW), BF16),
            pltpu.VMEM(rows, BF16),
            pltpu.VMEM(rows, BF16),
            pltpu.VMEM(rows, BF16),
            pltpu.VMEM(rows, BF16),
            pltpu.VMEM(rows, BF16),
            pltpu.VMEM(rows, BF16),
            pltpu.VMEM((8, 2, 4, HALF, R), BF16),
            pltpu.VMEM((8, 2, 2, HALF, R), BF16),
            pltpu.VMEM((8, NEAR, R), BF16),
            pltpu.VMEM((8, FAR, R), BF16),
            pltpu.VMEM((8, 2, HALF, R), BF16),
            pltpu.VMEM((2, UNIT, R), BF16),
            pltpu.VMEM((2 * T, R), F32),
            pltpu.VMEM((2 * T, R), F32),
            pltpu.VMEM((2 * T, 1), F32),
            pltpu.VMEM((2 * T, R), BF16),
            pltpu.VMEM((2, T, R), F32),
            pltpu.VMEM((2 * T, R), BF16),
            pltpu.VMEM((2, T, 1), F32),
            pltpu.VMEM((2, T, 1), F32),
            pltpu.VMEM((3, 8, R), F32),
            pltpu.VMEM((7, 8, R), F32),
            dma((64,)), dma((64,)),
            dma((4,)), dma((4,)),
            dma((64,)), dma((64,)),
            dma((ROWS,)), dma((ROWS,)),
            dma((ROWS,)), dma((ROWS,)),
            dma((7,)), dma((7,)),
            dma((5,)), dma((2,)),
            pltpu.SemaphoreType.REGULAR,
        ],
        compiler_params=pltpu.CompilerParams(
            collective_id=0, has_side_effects=True, vmem_limit_bytes=60 * 1024 * 1024
        ),
        name="relay",
    )(
        inflow[0], entering[0], arrive_grad[0], enter_grad[0], stashed[0],
        w_down[0], w_up[0].T, norm_gain, latent_gain,
    )
    outs = pl.pallas_call(
        finish,
        out_shape=(
            jax.ShapeDtypeStruct((T, D), BF16),
            jax.ShapeDtypeStruct((T, D), BF16),
            jax.ShapeDtypeStruct((UNIT, R), F32),
            jax.ShapeDtypeStruct((UNIT, R), F32),
            jax.ShapeDtypeStruct((1, UNIT), F32),
            jax.ShapeDtypeStruct((1, 8), F32),
        ),
        in_specs=[anyspace] * 2 + [vmem] * 5,
        out_specs=(anyspace,) * 2 + (vmem,) * 4,
        scratch_shapes=[dma((2,)), pltpu.VMEM((R, R), F32)],
        name="finish",
    )(acts, grads, down, up, lg, w_down[0], norm_gain)
    acts, grads, down, up, gin, glat = outs
    return acts[None], grads[None], down[None], up.T[None], gin, glat


def solution(mesh):
    in_specs = (
        P("section", "dp", None),
        P(None, "dp", None),
        P("section", "dp", None),
        P(None, "dp", None),
        P("section", "dp", None),
        P("section", "dp", None),
        P("section", None, "dp"),
        P("section", None),
        P("section", None),
    )
    out_specs = (
        P("section", "dp", None),
        P("section", "dp", None),
        P("section", "dp", None),
        P("section", None, "dp"),
        P("section", "dp"),
        P("section", "dp"),
    )
    return jax.shard_map(
        on_device, mesh=mesh, in_specs=in_specs, out_specs=out_specs, check_vma=False
    )
```

```python
import functools

import jax
import jax.numpy as jnp
from jax import lax
from jax.experimental import pallas as pl
from jax.experimental.pallas import tpu as pltpu
from jax.sharding import PartitionSpec as P

EPS = 1e-06
MESH = pl.DeviceIdType.MESH
F32 = jnp.float32
BF16 = jnp.bfloat16

D = 7168
R = 256
T = 128
UNIT = 224
HALF = 112
NEAR = 64
FAR = HALF - NEAR
ROW = 4 * UNIT
ROWS = D // ROW


def nt(a, b):
    return lax.dot_general(a, b, (((1,), (1,)), ((), ())), preferred_element_type=F32)


def tn(a, b):
    return lax.dot_general(a, b, (((0,), (0,)), ((), ())), preferred_element_type=F32)


def nn(a, b):
    return jnp.dot(a, b, preferred_element_type=F32)


def kernel(
    inflow, entering, arrive, enter, stashed, wd_in, wu_in, gin, glat,
    out_act, out_grad, out_down, out_up, out_lg,
    W, G, X, N, NT, GG, A1, N1, R0, B0, OA, OB,
    land_a, land_b, landn, landf, landu, land1, landz,
    LAT, LN, LS, LO, LO1, GL, RAW, MT, SC, LGP, LGL,
    gsend, grecv, zsend, zrecv, rsend, rrecv, asend, arecv, bsend, brecv,
    lsend, lrecv, isem, osem,
):
    s = lax.axis_index("section")
    d = lax.axis_index("dp")
    zh = d // 16
    x = (d // 4) % 4
    y = d % 4
    other = 1 - zh
    core = s % 2
    not_last = s < 7
    not_first = s > 0

    def dp_of(zz, xx, yy):
        return zz * 16 + xx * 4 + yy

    def along(axis, k):
        if axis == 0:
            return (s, dp_of(zh, (x + k) % 4, y))
        return (s, dp_of(zh, x, (y + k) % 4))

    partner = (s, dp_of(other, x, y))
    up_dev = (s + 1, d)
    down_dev = (s - 1, d)

    def remote(src, dst, ssem, rsem, dev):
        return pltpu.make_async_remote_copy(
            src_ref=src, dst_ref=dst, send_sem=ssem, recv_sem=rsem, device_id=dev, device_id_type=MESH
        )

    wcopy = [
        pltpu.make_async_copy(ref, W.at[m, zh, x, y], isem.at[m]) for m, ref in enumerate((wd_in, wu_in))
    ]
    for c in wcopy:
        c.start()

    def col(c):
        return pl.ds(pl.multiple_of(c * ROW, 128), ROW)

    def load_start(src, dst_of, sem):
        @pl.loop(0, ROWS)
        def _(c):
            pltpu.make_async_copy(src.at[:, col(c)], dst_of(c), sem).start()

    load_start(stashed, lambda c: X.at[0, c], isem.at[2])
    load_start(inflow, lambda c: X.at[1, c], isem.at[3])
    load_start(arrive, lambda c: GG.at[c, pl.ds(0, T)], isem.at[4])

    barrier = pltpu.get_barrier_semaphore()
    peers = [along(ax, k) for ax in (0, 1) for k in (1, 2, 3)] + [partner]
    peers += [((s + 1) % 8, d), ((s + 7) % 8, d)]
    for dev in peers:
        pl.semaphore_signal(barrier, inc=1, device_id=dev, device_id_type=MESH)
    pl.semaphore_wait(barrier, len(peers))

    @pl.when(s == 0)
    def _():
        @pl.loop(0, ROWS)
        def _(c):
            pltpu.make_async_copy(entering.at[:, col(c)], A1.at[c], arecv.at[c]).start()

    @pl.when(s == 7)
    def _():
        @pl.loop(0, ROWS)
        def _(c):
            pltpu.make_async_copy(enter.at[:, col(c)], GG.at[c, pl.ds(T, T)], brecv.at[c]).start()

    for c in wcopy:
        c.wait()

    def wreg(m, zz, h, i1, i2):
        rows = pl.ds(HALF * h, HALF)
        return W.at[m, zz, i2, i1, rows] if h == 0 else W.at[m, zz, i1, i2, rows]

    def gmsg(m, w, h, i, into=False):
        zz = zh if w == 0 else other
        a1, o1, a2, o2 = (1, y, 0, x) if h == 0 else (0, x, 1, y)
        n2, p2, f2 = (o2 + 3) % 4, (o2 + 1) % 4, (o2 + 2) % 4
        k = i + 1 if i < 3 else (i - 3) % 4
        unit = (o1 + (0, 3, 1, 2)[k]) % 4
        if i < 3:
            src, land, axis, step = (o1, o2), (unit, o2), a1, (1, 3, 2)[i]
        elif i < 7:
            src, land, axis, step = (unit, o2), (unit, n2), a2, 1
        elif i < 11:
            src, land, axis, step = (unit, o2), (unit, p2), a2, 3
        elif k in (0, 3):
            src, land, axis, step = (unit, n2), (unit, f2), a2, 1
        else:
            src, land, axis, step = (unit, p2), (unit, f2), a2, 3
        idx = ((m * 2 + w) * 2 + h) * 15 + i
        ref = wreg(m, zz, h, *(land if into else src))
        return remote(ref, ref, gsend.at[idx], grecv.at[idx], along(axis, step))

    def g_start(m, w):
        for i in (0, 1, 2, 3, 7):
            for h in (0, 1):
                gmsg(m, w, h, i).start()

    def g_first(m, w):
        for k in (1, 2, 3):
            for h in (0, 1):
                gmsg(m, w, h, k - 1, True).wait_recv()
                gmsg(m, w, h, 3 + k).start()
                gmsg(m, w, h, 7 + k).start()

    def g_second(m, w, ks=(0, 1, 2, 3)):
        for k in ks:
            for h in (0, 1):
                gmsg(m, w, h, (3 if k in (0, 3) else 7) + k, True).wait_recv()
                gmsg(m, w, h, 11 + k).start()

    def g_done(m, w):
        for k in range(4):
            for h in (0, 1):
                gmsg(m, w, h, (7 if k in (0, 3) else 3) + k, True).wait_recv()
                gmsg(m, w, h, 11 + k, True).wait_recv()

    def zcopy(m):
        own = W.at[m, zh, x, y]
        return remote(own, own, zsend.at[m], zrecv.at[m], partner)

    def zwait(m):
        far = W.at[m, other, x, y]
        remote(far, far, zsend.at[m], zrecv.at[m], partner).wait_recv()

    def gain(c):
        return gin[:, col(c)]

    def norms(src_of, scale_of, dst_of):
        def sq(c, acc):
            v = src_of(c)[...].astype(F32)
            return acc + jnp.sum(v * v, axis=-1, keepdims=True)

        total = lax.fori_loop(0, ROWS, sq, jnp.zeros((T, 1), F32))
        scale_of()[...] = lax.rsqrt(total * (1.0 / D) + EPS)

        @pl.loop(0, ROWS)
        def _(c):
            dst_of(c)[...] = (src_of(c)[...].astype(F32) * scale_of()[...] * gain(c)).astype(BF16)

    def wrow(m, zz, xx):
        return W[m, zz, xx].reshape(ROW, R)

    def latent_half(zz, rows_of, acc):
        @pl.loop(0, 4)
        def _(xx):
            acc[...] += nn(rows_of(zz * 4 + xx), wrow(0, zz, xx))

    def grad_lat_half(zz, k):
        @pl.loop(0, 4)
        def _(xx):
            GL[k] += nn(GG[zz * 4 + xx, pl.ds(k * T, T)], wrow(1, zz, xx))

    def raw_grad(k):
        rows = pl.ds(k * T, T)
        gl, ln, ls = GL[k], LN[rows], LS[rows]
        gn = gl * glat[...]
        m = jnp.mean(gn * ln, axis=-1, keepdims=True)
        raw = (ls * (gn - ln * m)).astype(BF16)
        RAW[rows] = raw
        MT[k] = jnp.sum(raw.astype(F32) * LAT[rows], axis=-1, keepdims=True) * (1.0 / D)
        LGP[0] += jnp.broadcast_to(jnp.sum(gl * ln, axis=0, keepdims=True), (8, R))

    def back_row(k, zz, xx):
        c = zz * 4 + xx
        grad_in = nt(RAW[pl.ds(k * T, T)], wrow(0, zz, xx)) * gain(c)
        sc = SC[k]
        in_norm = X[k, c].astype(F32) * sc
        g = GG[c, pl.ds(k * T, T)].astype(F32)
        return (g + sc * (grad_in - in_norm * MT[k])).astype(BF16)

    def act_copy(c):
        return remote(R0.at[c], A1.at[c], asend.at[c], arecv.at[c], up_dev)

    def back_copy(c):
        return remote(B0.at[c], GG.at[c, pl.ds(T, T)], bsend.at[c], brecv.at[c], down_dev)

    def result_half(zz):
        @pl.loop(0, 4)
        def _(xx):
            c = zz * 4 + xx
            R0[c] = (X[1, c].astype(F32) + nt(LO[pl.ds(T, T)], wrow(1, zz, xx))).astype(BF16)

            @pl.when(not_last)
            def _():
                act_copy(c).start()

    def send_back_half(zz):
        def body(k, zz, xx):
            c = zz * 4 + xx
            B0[c] = back_row(0, zz, xx)

            @pl.when(not_first)
            def _():
                back_copy(c).start()

        in_order(zz, body)

    OFF = (2, 1, 3, 0)
    POS, NEG = (0, 3), (1, 2)

    def greg(m, zz, h, i1, i2, r0=0, nr=HALF):
        rows = pl.ds(HALF * h + r0, nr)
        return G.at[m, zz, i1, i2, rows] if h == 0 else G.at[m, zz, i2, i1, rows]

    def r_ctx(m, w, h):
        zz = other if w == 0 else zh
        a1, o1, a2, o2 = (0, x, 1, y) if h == 0 else (1, y, 0, x)
        g = functools.partial(greg, m, zz, h)
        return g, a1, o1, a2, [(o2 + k) % 4 for k in OFF], (m * 2 + w) * 2 + h

    def rmsg(m, w, h, i):
        g, a1, o1, a2, j, q = r_ctx(m, w, h)
        u = i % 4
        if i < 4:
            src, land, axis, k = g((o1 + 2) % 4, j[u]), land_a.at[q, u], a1, 1 if u in POS else 3
        elif i < 8:
            src, land, axis, k = g((o1 + 1) % 4, j[u]), land_b.at[q, 0, u], a1, 1
        elif i < 12:
            src, land, axis, k = g((o1 + 3) % 4, j[u]), land_b.at[q, 1, u], a1, 3
        elif i == 12 and m == 0:
            src, land, axis, k = g(o1, j[0]), landu.at[q], a2, 2
        elif i == 12:
            src, land, axis, k = g(o1, j[0], 0, NEAR), landn.at[q], a2, 1
        elif i == 13:
            src, land, axis, k = g(o1, j[0], NEAR, FAR), landf.at[q], a2, 3
        elif i == 14:
            src, land, axis, k = g(o1, j[1]), land1.at[q, 0], a2, 1
        else:
            src, land, axis, k = g(o1, j[2]), land1.at[q, 1], a2, 3
        return remote(src, land, rsend.at[q * 16 + i], rrecv.at[q * 16 + i], along(axis, k))

    def add_into(ref, *lands):
        total = ref[...].astype(F32)
        for land in lands:
            total = total + land[...].astype(F32)
        ref[...] = total.astype(BF16)

    def r_row(m, w, k):
        if k == 0:
            for u in range(4):
                rmsg(m, w, 0, u).start()
        if k == 1:
            for u in NEG:
                rmsg(m, w, 0, 4 + u).start()
        if k == 2:
            for u in POS:
                rmsg(m, w, 0, 8 + u).start()
        rmsg(m, w, 1, k).start()
        rmsg(m, w, 1, (8 if k in POS else 4) + k).start()

    def r_relay(m, w, us=(0, 1, 2, 3)):
        for u in us:
            for h in (0, 1):
                g, a1, o1, a2, j, q = r_ctx(m, w, h)
                rmsg(m, w, h, u).wait_recv()
                add_into(g((o1 + (1 if u in POS else 3)) % 4, j[u]), land_a.at[q, u])
                rmsg(m, w, h, (4 if u in POS else 8) + u).start()

    def r_own(m, w, us):
        for u in us:
            for h in (0, 1):
                g, a1, o1, a2, j, q = r_ctx(m, w, h)
                rmsg(m, w, h, 4 + u).wait_recv()
                rmsg(m, w, h, 8 + u).wait_recv()
                add_into(g(o1, j[u]), land_b.at[q, 0, u], land_b.at[q, 1, u])
                if u == 0:
                    rmsg(m, w, h, 12).start()
                if u == 0 and m == 1:
                    rmsg(m, w, h, 13).start()
                if u in (1, 2) and m == 0:
                    rmsg(m, w, h, 13 + u).start()

    def r_ids(m):
        return [i for i in range(16) if m == 1 or i != 13]

    def r_relay2(m, w):
        for h in (0, 1):
            g, a1, o1, a2, j, q = r_ctx(m, w, h)
            rmsg(m, w, h, 12).wait_recv()
            add_into(g(o1, j[1], 0, NEAR), landn.at[q])
            rmsg(m, w, h, 14).start()
            rmsg(m, w, h, 13).wait_recv()
            add_into(g(o1, j[2], NEAR, FAR), landf.at[q])
            rmsg(m, w, h, 15).start()

    def zgrad(m):
        return remote(G.at[m, other, x, y], landz.at[m], zsend.at[2 + m], zrecv.at[2 + m], partner)

    def r_done(m, w):
        for h in (0, 1):
            g, a1, o1, a2, j, q = r_ctx(m, w, h)
            rmsg(m, w, h, 14).wait_recv()
            rmsg(m, w, h, 15).wait_recv()
            if m == 0:
                rmsg(m, w, h, 12).wait_recv()
            if w == 0:
                far = (landu.at[q],) if m == 0 else ()
                add_into(g(o1, j[3]), land1.at[q, 0], land1.at[q, 1], *far)
        if w == 0:
            zgrad(m).start()
        else:
            zgrad(m).wait_recv()
            out = out_down if m == 0 else out_up
            for h in (0, 1):
                g, a1, o1, a2, j, q = r_ctx(m, w, h)
                rows = pl.ds(HALF * h, HALF)
                total = g(o1, j[3])[...].astype(F32) + landz[m, rows].astype(F32)
                if m == 0:
                    total = total + landu[q].astype(F32)
                out[rows] = total + land1[q, 0].astype(F32) + land1[q, 1].astype(F32)

    def in_order(zz, body):
        @pl.loop(0, 4)
        def _(k):
            body(k, zz, (x + 2 + 3 * k + 3 * (k * (k - 1) // 2)) % 4)

    def after(k, w, m, extra):
        for i in range(4):

            @pl.when(k == i)
            def _():
                r_row(m, w, i)
                for step in extra.get(i, ()):
                    step()

    def up_half(w, extra):
        def body(k, zz, xx):
            c = zz * 4 + xx
            back_copy(c).wait_recv()
            G[1, zz, xx] = tn(GG[c], LO[...]).astype(BF16).reshape(4, UNIT, R)
            after(k, w, 1, extra)
            GL[1] += nn(GG[c, pl.ds(T, T)], wrow(1, zz, xx))

        in_order(other if w == 0 else zh, body)

    def down_half(w, extra):
        def body(k, zz, xx):
            G[0, zz, xx] = nn(NT[zz * 4 + xx], RAW[...]).astype(BF16).reshape(4, UNIT, R)
            after(k, w, 0, extra)

        in_order(other if w == 0 else zh, body)

    def transpose_rows():
        @pl.loop(0, ROWS)
        def _(c):
            NT[c] = N[c].T

    def out_copy(src, dst, c, sem):
        return pltpu.make_async_copy(src.at[c], dst.at[:, col(c)], sem)

    def out_back_half(zz):
        @pl.loop(0, 4)
        def _(xx):
            c = zz * 4 + xx
            OB[c] = back_row(1, zz, xx)
            out_copy(OB, out_grad, c, osem.at[1]).start()

    def lmsg(i):
        axis, k = ((1, 1), (1, 2), (1, 3), (0, 1), (0, 2), (0, 3), (None, 0))[i]
        dev = partner if axis is None else along(axis, k)
        stage = 0 if i < 3 else 1 if i < 6 else 2
        return remote(LGP.at[stage], LGL.at[i], lsend.at[i], lrecv.at[i], dev)

    def lg_start():
        for i in (0, 1, 2):
            lmsg(i).start()

    def lg_stage(stage):
        ids = ((0, 1, 2), (3, 4, 5), (6,))[stage]
        total = LGP[stage]
        for i in ids:
            lmsg(i).wait_recv()
            total = total + LGL[i]
        if stage == 2:
            out_lg[...] = total
        else:
            LGP[stage + 1] = total
            for i in ((3, 4, 5), (6,))[stage]:
                lmsg(i).start()

    def next_norms():
        @pl.loop(0, ROWS)
        def _(c):
            act_copy(c).wait_recv()

        norms(lambda c: A1.at[c], lambda: SC.at[0], lambda c: N1.at[c])

    def next_latent():
        GL[0] = jnp.zeros((T, R), F32)
        latent_half(zh, lambda c: N1[c], GL.at[0])
        latent_half(other, lambda c: N1[c], GL.at[0])
        lat1 = GL[0]
        LO1[...] = (
            lat1 * lax.rsqrt(jnp.mean(lat1 * lat1, axis=-1, keepdims=True) + EPS) * glat[...]
        ).astype(BF16)

    def next_result():
        @pl.loop(0, ROWS)
        def _(c):
            OA[c] = (A1[c].astype(F32) + nt(LO1[...], wrow(1, c // 4, c % 4))).astype(BF16)
            out_copy(OA, out_act, c, osem.at[0]).start()

    def z_start():
        for m in (0, 1):
            zcopy(m).start()

    z_start()
    g_start(0, 0)
    g_start(1, 0)
    LAT[...] = jnp.zeros_like(LAT)
    GL[...] = jnp.zeros_like(GL)
    LGP[0] = jnp.zeros((8, R), F32)
    pltpu.make_async_copy(X.at[0], X.at[0], isem.at[2]).wait()
    norms(lambda c: X.at[0, c], lambda: SC.at[0], lambda c: N.at[c, pl.ds(0, T)])
    g_first(0, 0)
    g_first(1, 0)
    g_second(0, 0, (0,))
    g_second(1, 0, (0,))
    pltpu.make_async_copy(X.at[1], X.at[1], isem.at[3]).wait()
    norms(lambda c: X.at[1, c], lambda: SC.at[1], lambda c: N.at[c, pl.ds(T, T)])
    g_second(0, 0, (1, 2, 3))
    g_second(1, 0, (1, 2, 3))
    zwait(0)
    g_start(0, 1)
    zwait(1)
    g_start(1, 1)
    g_first(0, 1)
    g_first(1, 1)
    transpose_rows()
    g_done(0, 0)
    latent_half(zh, lambda c: N[c], LAT)
    g_second(0, 1)
    g_done(1, 0)
    first_half = GG.at[:, pl.ds(0, T)]
    pltpu.make_async_copy(first_half, first_half, isem.at[4]).wait()
    grad_lat_half(zh, 0)
    g_second(1, 1)
    g_done(0, 1)
    latent_half(other, lambda c: N[c], LAT)
    lat = LAT[...]
    lat_scale = lax.rsqrt(jnp.mean(lat * lat, axis=-1, keepdims=True) + EPS)
    LS[...] = lat_scale
    LN[...] = lat * lat_scale
    LO[...] = (lat * lat_scale * glat[...]).astype(BF16)
    result_half(zh)
    g_done(1, 1)
    grad_lat_half(other, 0)
    raw_grad(0)
    send_back_half(other)
    send_back_half(zh)
    result_half(other)

    def do(f, *args):
        return lambda: f(*args)

    @pl.when(core == 0)
    def _():
        up_half(0, {})
        up_half(1, {})
        r_relay(1, 0)
        raw_grad(1)
        lg_start()
        down_half(0, {})
        r_relay(1, 1)
        r_own(1, 0, (0, 1, 2))
        down_half(1, {})
        r_relay2(1, 0)
        r_relay(0, 0)
        r_own(1, 1, (0, 1, 2))
        r_own(1, 0, (3,))
        r_relay(0, 1)
        r_relay2(1, 1)
        r_done(1, 0)
        r_own(0, 0, (0, 1, 2))
        lg_stage(0)
        r_own(1, 1, (3,))
        r_own(0, 1, (0, 1, 2))
        r_own(0, 0, (3,))
        r_done(0, 0)
        lg_stage(1)
        out_back_half(other)
        r_done(1, 1)
        r_own(0, 1, (3,))
        out_back_half(zh)
        next_norms()
        next_latent()
        next_result()
        lg_stage(2)
        r_done(0, 1)

    @pl.when(core == 1)
    def _():
        up_half(0, {})
        next_norms()
        next_latent()
        next_result()
        up_half(1, {
            0: [do(r_relay, 1, 0)],
            1: [do(r_own, 1, 0, (0, 1))],
            2: [do(r_own, 1, 0, (2,)), do(r_relay2, 1, 0)],
            3: [do(r_own, 1, 0, (3,))],
        })
        raw_grad(1)
        lg_start()
        down_half(0, {})
        r_relay(1, 1)
        down_half(1, {})
        r_done(1, 0)
        r_relay(0, 0)
        r_own(1, 1, (0, 1, 2))
        r_own(0, 0, (0, 1, 2))
        r_relay(0, 1)
        r_relay2(1, 1)
        r_own(0, 0, (3,))
        r_done(0, 0)
        lg_stage(0)
        r_own(0, 1, (0, 1, 2))
        r_own(1, 1, (3,))
        out_back_half(other)
        lg_stage(1)
        r_own(0, 1, (3,))
        r_done(1, 1)
        out_back_half(zh)
        lg_stage(2)
        r_done(0, 1)

    for m in (0, 1):
        zcopy(m).wait_send()
        zgrad(m).wait_send()
        for w in (0, 1):
            for h in (0, 1):
                for i in range(15):
                    gmsg(m, w, h, i).wait_send()
                for i in r_ids(m):
                    rmsg(m, w, h, i).wait_send()
    for i in range(7):
        lmsg(i).wait_send()

    @pl.when(not_last)
    def _():
        @pl.loop(0, ROWS)
        def _(c):
            act_copy(c).wait_send()

    @pl.when(not_first)
    def _():
        @pl.loop(0, ROWS)
        def _(c):
            back_copy(c).wait_send()

    pltpu.make_async_copy(OA, OA, osem.at[0]).wait()
    pltpu.make_async_copy(OB, OB, osem.at[1]).wait()


def finish(acts, grads, down, up, lg, wd, gain, o_acts, o_grads, o_down, o_up, o_gin, o_glat, pad):
    d = lax.axis_index("dp")
    o_acts[...] = acts[...]
    o_grads[...] = grads[...]

    @pl.when(pl.program_id(0) == 0)
    def _():
        o_down[...] = down[...]
        o_up[...] = up[...]
        pad[pl.ds(0, UNIT)] = down[...] * wd[...].astype(F32)
        pad[pl.ds(UNIT, R - UNIT)] = jnp.zeros((R - UNIT, R), F32)
        sums = jnp.sum(pad[...].T, axis=0, keepdims=True)
        first = d * UNIT
        start = pl.multiple_of(jnp.minimum(first // 128 * 128, D - 384), 128)
        window = jnp.broadcast_to(gain[:, pl.ds(start, 384)], (8, 384))
        own = pltpu.roll(window, (384 - (first - start)) % 384, 1)
        o_gin[...] = sums[:, :UNIT] / own[0:1, :UNIT]
        o_glat[...] = pltpu.roll(lg[...], (R - 8 * d) % R, 1)[0:1, :8]


def on_device(
    inflow, entering, arrive_grad, enter_grad, stashed, w_down, w_up, norm_gain, latent_gain
):
    anyspace = pl.BlockSpec(memory_space=pl.ANY)
    vmem = pl.BlockSpec(memory_space=pltpu.VMEM)
    block = pl.BlockSpec((T // 4, D), lambda i: (i, 0))
    rows = (ROWS, T, ROW)
    dma = pltpu.SemaphoreType.DMA
    acts, grads, down, up, lg = pl.pallas_call(
        kernel,
        out_shape=(
            jax.ShapeDtypeStruct((T, D), BF16),
            jax.ShapeDtypeStruct((T, D), BF16),
            jax.ShapeDtypeStruct((UNIT, R), F32),
            jax.ShapeDtypeStruct((UNIT, R), F32),
            jax.ShapeDtypeStruct((8, R), F32),
        ),
        in_specs=[anyspace] * 7 + [vmem] * 2,
        out_specs=(anyspace, anyspace, vmem, vmem, vmem),
        scratch_shapes=[
            pltpu.VMEM((2, 2, 4, 4, UNIT, R), BF16),
            pltpu.VMEM((2, 2, 4, 4, UNIT, R), BF16),
            pltpu.VMEM((2,) + rows, BF16),
            pltpu.VMEM((ROWS, 2 * T, ROW), BF16),
            pltpu.VMEM((ROWS, ROW, 2 * T), BF16),
            pltpu.VMEM((ROWS, 2 * T, ROW), BF16),
            pltpu.VMEM(rows, BF16),
            pltpu.VMEM(rows, BF16),
            pltpu.VMEM(rows, BF16),
            pltpu.VMEM(rows, BF16),
            pltpu.VMEM(rows, BF16),
            pltpu.VMEM(rows, BF16),
            pltpu.VMEM((8, 4, HALF, R), BF16),
            pltpu.VMEM((8, 2, 4, HALF, R), BF16),
            pltpu.VMEM((8, NEAR, R), BF16),
            pltpu.VMEM((8, FAR, R), BF16),
            pltpu.VMEM((4, HALF, R), BF16),
            pltpu.VMEM((8, 2, HALF, R), BF16),
            pltpu.VMEM((2, UNIT, R), BF16),
            pltpu.VMEM((2 * T, R), F32),
            pltpu.VMEM((2 * T, R), F32),
            pltpu.VMEM((2 * T, 1), F32),
            pltpu.VMEM((2 * T, R), BF16),
            pltpu.VMEM((T, R), BF16),
            pltpu.VMEM((2, T, R), F32),
            pltpu.VMEM((2 * T, R), BF16),
            pltpu.VMEM((2, T, 1), F32),
            pltpu.VMEM((2, T, 1), F32),
            pltpu.VMEM((3, 8, R), F32),
            pltpu.VMEM((7, 8, R), F32),
            dma((120,)), dma((120,)),
            dma((4,)), dma((4,)),
            dma((128,)), dma((128,)),
            dma((ROWS,)), dma((ROWS,)),
            dma((ROWS,)), dma((ROWS,)),
            dma((7,)), dma((7,)),
            dma((5,)), dma((2,)),
        ],
        compiler_params=pltpu.CompilerParams(
            collective_id=0, has_side_effects=True, vmem_limit_bytes=60 * 1024 * 1024
        ),
        name="relay",
    )(
        inflow[0], entering[0], arrive_grad[0], enter_grad[0], stashed[0],
        w_down[0], w_up[0].T, norm_gain, latent_gain,
    )
    outs = pl.pallas_call(
        finish,
        out_shape=(
            jax.ShapeDtypeStruct((T, D), BF16),
            jax.ShapeDtypeStruct((T, D), BF16),
            jax.ShapeDtypeStruct((UNIT, R), F32),
            jax.ShapeDtypeStruct((UNIT, R), F32),
            jax.ShapeDtypeStruct((1, UNIT), F32),
            jax.ShapeDtypeStruct((1, 8), F32),
        ),
        grid=(4,),
        in_specs=[block, block] + [vmem] * 5,
        out_specs=(block, block) + (vmem,) * 4,
        scratch_shapes=[pltpu.VMEM((R, R), F32)],
        name="finish",
    )(acts, grads, down, up, lg, w_down[0], norm_gain)
    acts, grads, down, up, gin, glat = outs
    return acts[None], grads[None], down[None], up.T[None], gin, glat


def solution(mesh):
    in_specs = (
        P("section", "dp", None),
        P(None, "dp", None),
        P("section", "dp", None),
        P(None, "dp", None),
        P("section", "dp", None),
        P("section", "dp", None),
        P("section", None, "dp"),
        P("section", None),
        P("section", None),
    )
    out_specs = (
        P("section", "dp", None),
        P("section", "dp", None),
        P("section", "dp", None),
        P("section", None, "dp"),
        P("section", "dp"),
        P("section", "dp"),
    )
    return jax.shard_map(
        on_device, mesh=mesh, in_specs=in_specs, out_specs=out_specs, check_vma=False
    )
```

```python
import functools

import jax
import jax.numpy as jnp
from jax import lax
from jax.experimental import pallas as pl
from jax.experimental.pallas import tpu as pltpu
from jax.sharding import PartitionSpec as P

EPS = 1e-06
MESH = pl.DeviceIdType.MESH
F32 = jnp.float32
BF16 = jnp.bfloat16

D = 7168
R = 256
T = 128
UNIT = 224
HALF = 112
NEAR = 64
FAR = HALF - NEAR
ROW = 4 * UNIT
ROWS = D // ROW


def nt(a, b):
    return lax.dot_general(a, b, (((1,), (1,)), ((), ())), preferred_element_type=F32)


def tn(a, b):
    return lax.dot_general(a, b, (((0,), (0,)), ((), ())), preferred_element_type=F32)


def nn(a, b):
    return jnp.dot(a, b, preferred_element_type=F32)


def kernel(
    inflow, entering, arrive, enter, stashed, wd_in, wu_in, gin, glat,
    out_act, out_grad, out_down, out_up, out_lg,
    W, G, X, N, NT, GG, A1, N1, R0, B0, OA, OB,
    land_a, land_b, landn, landf, landu, land1, landz,
    LAT, LN, LS, LO, LO1, GL, RAW, MT, SC, LGP, LGL,
    gsend, grecv, zsend, zrecv, rsend, rrecv, asend, arecv, bsend, brecv,
    lsend, lrecv, isem, osem, go,
):
    s = lax.axis_index("section")
    d = lax.axis_index("dp")
    zh = d // 16
    x = (d // 4) % 4
    y = d % 4
    other = 1 - zh
    core = s % 2
    not_last = s < 7
    not_first = s > 0

    def dp_of(zz, xx, yy):
        return zz * 16 + xx * 4 + yy

    def along(axis, k):
        if axis == 0:
            return (s, dp_of(zh, (x + k) % 4, y))
        return (s, dp_of(zh, x, (y + k) % 4))

    partner = (s, dp_of(other, x, y))
    up_dev = (s + 1, d)
    down_dev = (s - 1, d)

    def remote(src, dst, ssem, rsem, dev):
        return pltpu.make_async_remote_copy(
            src_ref=src, dst_ref=dst, send_sem=ssem, recv_sem=rsem, device_id=dev, device_id_type=MESH
        )

    barrier = pltpu.get_barrier_semaphore()
    peers = [along(ax, k) for ax in (0, 1) for k in (1, 2, 3)] + [partner]
    peers += [((s + 1) % 8, d), ((s + 7) % 8, d)]
    for dev in peers:
        pl.semaphore_signal(barrier, inc=1, device_id=dev, device_id_type=MESH)

    wcopy = [
        pltpu.make_async_copy(ref, W.at[m, zh, x, y], isem.at[m]) for m, ref in enumerate((wd_in, wu_in))
    ]
    for c in wcopy:
        c.start()

    def col(c):
        return pl.ds(pl.multiple_of(c * ROW, 128), ROW)

    def load_start(src, dst_of, sem):
        @pl.loop(0, ROWS)
        def _(c):
            pltpu.make_async_copy(src.at[:, col(c)], dst_of(c), sem).start()

    load_start(stashed, lambda c: X.at[0, c], isem.at[2])
    load_start(inflow, lambda c: X.at[1, c], isem.at[3])
    load_start(arrive, lambda c: GG.at[c, pl.ds(0, T)], isem.at[4])

    pl.semaphore_wait(barrier, len(peers))

    @pl.when(s == 0)
    def _():
        @pl.loop(0, ROWS)
        def _(c):
            pltpu.make_async_copy(entering.at[:, col(c)], A1.at[c], arecv.at[c]).start()

    @pl.when(s == 7)
    def _():
        @pl.loop(0, ROWS)
        def _(c):
            pltpu.make_async_copy(enter.at[:, col(c)], GG.at[c, pl.ds(T, T)], brecv.at[c]).start()

    for c in wcopy:
        c.wait()

    def wreg(m, zz, h, i1, i2):
        rows = pl.ds(HALF * h, HALF)
        return W.at[m, zz, i2, i1, rows] if h == 0 else W.at[m, zz, i1, i2, rows]

    def gmsg(m, w, h, i, into=False):
        zz = zh if w == 0 else other
        a1, o1, a2, o2 = (1, y, 0, x) if h == 0 else (0, x, 1, y)
        n2, p2, f2 = (o2 + 3) % 4, (o2 + 1) % 4, (o2 + 2) % 4
        k = i + 1 if i < 3 else (i - 3) % 4
        unit = (o1 + (0, 3, 1, 2)[k]) % 4
        if i < 3:
            src, land, axis, step = (o1, o2), (unit, o2), a1, (1, 3, 2)[i]
        elif i < 7:
            src, land, axis, step = (unit, o2), (unit, n2), a2, 1
        elif i < 11:
            src, land, axis, step = (unit, o2), (unit, p2), a2, 3
        elif k in (0, 3):
            src, land, axis, step = (unit, n2), (unit, f2), a2, 1
        else:
            src, land, axis, step = (unit, p2), (unit, f2), a2, 3
        idx = ((m * 2 + w) * 2 + h) * 15 + i
        ref = wreg(m, zz, h, *(land if into else src))
        return remote(ref, ref, gsend.at[idx], grecv.at[idx], along(axis, step))

    def g_start(m, w):
        for i in (0, 1, 2, 3, 7):
            for h in (0, 1):
                gmsg(m, w, h, i).start()

    def g_first(m, w):
        for k in (1, 2, 3):
            for h in (0, 1):
                gmsg(m, w, h, k - 1, True).wait_recv()
                gmsg(m, w, h, 3 + k).start()
                gmsg(m, w, h, 7 + k).start()

    def g_second(m, w, ks=(0, 1, 2, 3)):
        for k in ks:
            for h in (0, 1):
                gmsg(m, w, h, (3 if k in (0, 3) else 7) + k, True).wait_recv()
                gmsg(m, w, h, 11 + k).start()

    def g_done(m, w):
        for k in range(4):
            for h in (0, 1):
                gmsg(m, w, h, (7 if k in (0, 3) else 3) + k, True).wait_recv()
                gmsg(m, w, h, 11 + k, True).wait_recv()

    def zcopy(m):
        own = W.at[m, zh, x, y]
        return remote(own, own, zsend.at[m], zrecv.at[m], partner)

    def zwait(m):
        far = W.at[m, other, x, y]
        remote(far, far, zsend.at[m], zrecv.at[m], partner).wait_recv()

    def gain(c):
        return gin[:, col(c)]

    def norms(src_of, scale_of, dst_of):
        def sq(c, acc):
            v = src_of(c)[...].astype(F32)
            return acc + jnp.sum(v * v, axis=-1, keepdims=True)

        total = lax.fori_loop(0, ROWS, sq, jnp.zeros((T, 1), F32))
        scale_of()[...] = lax.rsqrt(total * (1.0 / D) + EPS)

        @pl.loop(0, ROWS)
        def _(c):
            dst_of(c)[...] = (src_of(c)[...].astype(F32) * scale_of()[...] * gain(c)).astype(BF16)

    def wrow(m, zz, xx):
        return W[m, zz, xx].reshape(ROW, R)

    def latent_half(zz, rows_of, acc):
        @pl.loop(0, 4)
        def _(xx):
            acc[...] += nn(rows_of(zz * 4 + xx), wrow(0, zz, xx))

    def grad_lat_half(zz, k):
        @pl.loop(0, 4)
        def _(xx):
            GL[k] += nn(GG[zz * 4 + xx, pl.ds(k * T, T)], wrow(1, zz, xx))

    def raw_grad(k):
        rows = pl.ds(k * T, T)
        gl, ln, ls = GL[k], LN[rows], LS[rows]
        gn = gl * glat[...]
        m = jnp.mean(gn * ln, axis=-1, keepdims=True)
        raw = (ls * (gn - ln * m)).astype(BF16)
        RAW[rows] = raw
        MT[k] = jnp.sum(raw.astype(F32) * LAT[rows], axis=-1, keepdims=True) * (1.0 / D)
        LGP[0] += jnp.broadcast_to(jnp.sum(gl * ln, axis=0, keepdims=True), (8, R))

    def back_row(k, zz, xx):
        c = zz * 4 + xx
        grad_in = nt(RAW[pl.ds(k * T, T)], wrow(0, zz, xx)) * gain(c)
        sc = SC[k]
        in_norm = X[k, c].astype(F32) * sc
        g = GG[c, pl.ds(k * T, T)].astype(F32)
        return (g + sc * (grad_in - in_norm * MT[k])).astype(BF16)

    def act_copy(c):
        return remote(R0.at[c], A1.at[c], asend.at[c], arecv.at[c], up_dev)

    def back_copy(c):
        return remote(B0.at[c], GG.at[c, pl.ds(T, T)], bsend.at[c], brecv.at[c], down_dev)

    def result_half(zz):
        @pl.loop(0, 4)
        def _(xx):
            c = zz * 4 + xx
            R0[c] = (X[1, c].astype(F32) + nt(LO[pl.ds(T, T)], wrow(1, zz, xx))).astype(BF16)

            @pl.when(not_last)
            def _():
                act_copy(c).start()

    def send_back_half(zz):
        def body(k, zz, xx):
            c = zz * 4 + xx
            B0[c] = back_row(0, zz, xx)

            @pl.when(not_first)
            def _():
                back_copy(c).start()

        in_order(zz, body)

    OFF = (2, 1, 3, 0)
    POS, NEG = (0, 3), (1, 2)

    def greg(m, zz, h, i1, i2, r0=0, nr=HALF):
        rows = pl.ds(HALF * h + r0, nr)
        return G.at[m, zz, i1, i2, rows] if h == 0 else G.at[m, zz, i2, i1, rows]

    def r_ctx(m, w, h):
        zz = other if w == 0 else zh
        a1, o1, a2, o2 = (0, x, 1, y) if h == 0 else (1, y, 0, x)
        g = functools.partial(greg, m, zz, h)
        return g, a1, o1, a2, [(o2 + k) % 4 for k in OFF], (m * 2 + w) * 2 + h

    def rmsg(m, w, h, i):
        g, a1, o1, a2, j, q = r_ctx(m, w, h)
        u = i % 4
        if i < 4:
            src, land, axis, k = g((o1 + 2) % 4, j[u]), land_a.at[q, u], a1, 1 if u in POS else 3
        elif i < 8:
            src, land, axis, k = g((o1 + 1) % 4, j[u]), land_b.at[q, 0, u], a1, 1
        elif i < 12:
            src, land, axis, k = g((o1 + 3) % 4, j[u]), land_b.at[q, 1, u], a1, 3
        elif i == 12 and m == 0:
            src, land, axis, k = g(o1, j[0]), landu.at[q], a2, 2
        elif i == 12:
            src, land, axis, k = g(o1, j[0], 0, NEAR), landn.at[q], a2, 1
        elif i == 13:
            src, land, axis, k = g(o1, j[0], NEAR, FAR), landf.at[q], a2, 3
        elif i == 14:
            src, land, axis, k = g(o1, j[1]), land1.at[q, 0], a2, 1
        else:
            src, land, axis, k = g(o1, j[2]), land1.at[q, 1], a2, 3
        return remote(src, land, rsend.at[q * 16 + i], rrecv.at[q * 16 + i], along(axis, k))

    def add_into(ref, *lands):
        total = ref[...].astype(F32)
        for land in lands:
            total = total + land[...].astype(F32)
        ref[...] = total.astype(BF16)

    def r_row(m, w, k):
        if k == 0:
            for u in range(4):
                rmsg(m, w, 0, u).start()
        if k == 1:
            for u in NEG:
                rmsg(m, w, 0, 4 + u).start()
        if k == 2:
            for u in POS:
                rmsg(m, w, 0, 8 + u).start()
        rmsg(m, w, 1, k).start()
        rmsg(m, w, 1, (8 if k in POS else 4) + k).start()

    def r_relay(m, w, us=(0, 1, 2, 3)):
        for u in us:
            for h in (0, 1):
                g, a1, o1, a2, j, q = r_ctx(m, w, h)
                rmsg(m, w, h, u).wait_recv()
                add_into(g((o1 + (1 if u in POS else 3)) % 4, j[u]), land_a.at[q, u])
                rmsg(m, w, h, (4 if u in POS else 8) + u).start()

    def r_own(m, w, us=(0, 1, 2, 3)):
        for u in us:
            for h in (0, 1):
                g, a1, o1, a2, j, q = r_ctx(m, w, h)
                rmsg(m, w, h, 4 + u).wait_recv()
                rmsg(m, w, h, 8 + u).wait_recv()
                add_into(g(o1, j[u]), land_b.at[q, 0, u], land_b.at[q, 1, u])
                if u == 0:
                    rmsg(m, w, h, 12).start()
                if u == 0 and m == 1:
                    rmsg(m, w, h, 13).start()
                if u in (1, 2) and m == 0:
                    rmsg(m, w, h, 13 + u).start()

    def r_ids(m):
        return [i for i in range(16) if m == 1 or i != 13]

    def r_relay2(m, w):
        for h in (0, 1):
            g, a1, o1, a2, j, q = r_ctx(m, w, h)
            rmsg(m, w, h, 12).wait_recv()
            add_into(g(o1, j[1], 0, NEAR), landn.at[q])
            rmsg(m, w, h, 14).start()
            rmsg(m, w, h, 13).wait_recv()
            add_into(g(o1, j[2], NEAR, FAR), landf.at[q])
            rmsg(m, w, h, 15).start()

    def zgrad(m):
        return remote(G.at[m, other, x, y], landz.at[m], zsend.at[2 + m], zrecv.at[2 + m], partner)

    def r_done(m, w):
        for h in (0, 1):
            g, a1, o1, a2, j, q = r_ctx(m, w, h)
            rmsg(m, w, h, 14).wait_recv()
            rmsg(m, w, h, 15).wait_recv()
            if m == 0:
                rmsg(m, w, h, 12).wait_recv()
            if w == 0:
                far = (landu.at[q],) if m == 0 else ()
                add_into(g(o1, j[3]), land1.at[q, 0], land1.at[q, 1], *far)
        if w == 0:
            zgrad(m).start()
        else:
            zgrad(m).wait_recv()
            out = out_down if m == 0 else out_up
            for h in (0, 1):
                g, a1, o1, a2, j, q = r_ctx(m, w, h)
                rows = pl.ds(HALF * h, HALF)
                total = g(o1, j[3])[...].astype(F32) + landz[m, rows].astype(F32)
                if m == 0:
                    total = total + landu[q].astype(F32)
                out[rows] = total + land1[q, 0].astype(F32) + land1[q, 1].astype(F32)

    def in_order(zz, body):
        @pl.loop(0, 4)
        def _(k):
            body(k, zz, (x + 2 + 3 * k + 3 * (k * (k - 1) // 2)) % 4)

    def after(k, w, m, extra):
        for i in range(4):

            @pl.when(k == i)
            def _():
                r_row(m, w, i)
                for step in extra.get(i, ()):
                    step()

    def up_half(w, extra):
        def body(k, zz, xx):
            c = zz * 4 + xx
            back_copy(c).wait_recv()
            G[1, zz, xx] = tn(GG[c], LO[...]).astype(BF16).reshape(4, UNIT, R)
            after(k, w, 1, extra)
            GL[1] += nn(GG[c, pl.ds(T, T)], wrow(1, zz, xx))

        in_order(other if w == 0 else zh, body)

    def down_half(w, extra):
        def body(k, zz, xx):
            G[0, zz, xx] = nn(NT[zz * 4 + xx], RAW[...]).astype(BF16).reshape(4, UNIT, R)
            after(k, w, 0, extra)

        in_order(other if w == 0 else zh, body)

    def transpose_rows():
        @pl.loop(0, ROWS)
        def _(c):
            NT[c] = N[c].T

    def out_copy(src, dst, c, sem):
        return pltpu.make_async_copy(src.at[c], dst.at[:, col(c)], sem)

    def out_back_half(zz):
        @pl.loop(0, 4)
        def _(xx):
            c = zz * 4 + xx
            OB[c] = back_row(1, zz, xx)
            out_copy(OB, out_grad, c, osem.at[1]).start()

    def lmsg(i):
        axis, k = ((1, 1), (1, 2), (1, 3), (0, 1), (0, 2), (0, 3), (None, 0))[i]
        dev = partner if axis is None else along(axis, k)
        stage = 0 if i < 3 else 1 if i < 6 else 2
        return remote(LGP.at[stage], LGL.at[i], lsend.at[i], lrecv.at[i], dev)

    def lg_start():
        for i in (0, 1, 2):
            lmsg(i).start()

    def lg_stage(stage):
        ids = ((0, 1, 2), (3, 4, 5), (6,))[stage]
        total = LGP[stage]
        for i in ids:
            lmsg(i).wait_recv()
            total = total + LGL[i]
        if stage == 2:
            out_lg[...] = total
        else:
            LGP[stage + 1] = total
            for i in ((3, 4, 5), (6,))[stage]:
                lmsg(i).start()

    def next_norms():
        @pl.loop(0, ROWS)
        def _(c):
            act_copy(c).wait_recv()

        norms(lambda c: A1.at[c], lambda: SC.at[0], lambda c: N1.at[c])

    def next_latent():
        GL[0] = jnp.zeros((T, R), F32)
        latent_half(zh, lambda c: N1[c], GL.at[0])
        latent_half(other, lambda c: N1[c], GL.at[0])
        lat1 = GL[0]
        LO1[...] = (
            lat1 * lax.rsqrt(jnp.mean(lat1 * lat1, axis=-1, keepdims=True) + EPS) * glat[...]
        ).astype(BF16)

    def next_result():
        @pl.loop(0, ROWS)
        def _(c):
            OA[c] = (A1[c].astype(F32) + nt(LO1[...], wrow(1, c // 4, c % 4))).astype(BF16)
            out_copy(OA, out_act, c, osem.at[0]).start()

    def g_sent():
        for m in (0, 1):
            zcopy(m).wait_send()
            for w in (0, 1):
                for h in (0, 1):
                    for i in range(15):
                        gmsg(m, w, h, i).wait_send()

    def r_sent(m):
        for w in (0, 1):
            for h in (0, 1):
                for i in r_ids(m):
                    rmsg(m, w, h, i).wait_send()

    def up_sent():
        zgrad(1).wait_send()
        r_sent(1)

    def z_start():
        for m in (0, 1):
            zcopy(m).start()

    z_start()
    g_start(0, 0)
    g_start(1, 0)
    LAT[...] = jnp.zeros_like(LAT)
    GL[...] = jnp.zeros_like(GL)
    LGP[0] = jnp.zeros((8, R), F32)
    pltpu.make_async_copy(X.at[0], X.at[0], isem.at[2]).wait()
    norms(lambda c: X.at[0, c], lambda: SC.at[0], lambda c: N.at[c, pl.ds(0, T)])
    g_first(0, 0)
    g_first(1, 0)
    g_second(0, 0, (0,))
    g_second(1, 0, (0,))
    pltpu.make_async_copy(X.at[1], X.at[1], isem.at[3]).wait()
    norms(lambda c: X.at[1, c], lambda: SC.at[1], lambda c: N.at[c, pl.ds(T, T)])
    g_second(0, 0, (1, 2, 3))
    g_second(1, 0, (1, 2, 3))
    zwait(0)
    g_start(0, 1)
    zwait(1)

    @pl.when(core == 0)
    def _():
        g_start(1, 1)
        g_first(0, 1)
        g_first(1, 1)
        pl.semaphore_signal(go, inc=1, device_id=up_dev, device_id_type=MESH)

    @pl.when(core == 1)
    def _():
        g_first(0, 1)
        g_second(0, 1)
        transpose_rows()
        pl.semaphore_wait(go, 1)
        g_start(1, 1)
        g_first(1, 1)

    @pl.when(core == 0)
    def _():
        transpose_rows()
        g_second(0, 1)

    g_done(0, 0)
    latent_half(zh, lambda c: N[c], LAT)
    g_done(1, 0)
    first_half = GG.at[:, pl.ds(0, T)]
    pltpu.make_async_copy(first_half, first_half, isem.at[4]).wait()
    grad_lat_half(zh, 0)
    g_second(1, 1)
    g_done(0, 1)
    latent_half(other, lambda c: N[c], LAT)
    lat = LAT[...]
    lat_scale = lax.rsqrt(jnp.mean(lat * lat, axis=-1, keepdims=True) + EPS)
    LS[...] = lat_scale
    LN[...] = lat * lat_scale
    LO[...] = (lat * lat_scale * glat[...]).astype(BF16)
    result_half(zh)
    g_done(1, 1)
    grad_lat_half(other, 0)
    raw_grad(0)
    send_back_half(other)
    send_back_half(zh)

    def do(f, *args):
        return lambda: f(*args)

    @pl.when(core == 0)
    def _():
        up_half(0, {})
        up_half(1, {})
        result_half(other)
        r_relay(1, 0)
        raw_grad(1)
        lg_start()
        down_half(0, {})
        r_relay(1, 1)
        r_own(1, 0, (0, 1, 2))
        down_half(1, {})
        r_relay2(1, 0)
        r_relay(0, 0)
        r_own(1, 1, (0, 1, 2))
        r_own(1, 0, (3,))
        r_relay(0, 1)
        r_relay2(1, 1)
        r_done(1, 0)
        r_own(0, 0, (0, 1, 2))
        lg_stage(0)
        r_own(1, 1, (3,))
        r_own(0, 1, (0, 1, 2))
        r_own(0, 0, (3,))
        r_done(0, 0)
        lg_stage(1)
        out_back_half(other)
        r_done(1, 1)
        r_own(0, 1, (3,))
        out_back_half(zh)
        g_sent()
        up_sent()
        next_norms()
        next_latent()
        next_result()
        lg_stage(2)
        r_done(0, 1)

    @pl.when(core == 1)
    def _():
        result_half(other)
        up_half(0, {})
        next_norms()
        next_latent()
        next_result()
        g_sent()
        up_half(1, {
            0: [do(r_relay, 1, 0)],
            1: [do(r_own, 1, 0, (0, 1))],
            2: [do(r_own, 1, 0, (2,)), do(r_relay2, 1, 0)],
            3: [do(r_own, 1, 0, (3,))],
        })
        raw_grad(1)
        lg_start()
        down_half(0, {})
        r_relay(1, 1)
        down_half(1, {})
        r_done(1, 0)
        r_relay(0, 0)
        r_own(1, 1, (0, 1, 2))
        r_relay(0, 1)
        r_own(0, 0)
        r_relay2(1, 1)
        r_done(0, 0)
        lg_stage(0)
        r_own(0, 1)
        r_own(1, 1, (3,))
        lg_stage(1)
        out_back_half(other)
        r_done(1, 1)
        out_back_half(zh)
        up_sent()
        lg_stage(2)
        r_done(0, 1)

    zgrad(0).wait_send()
    r_sent(0)
    for i in range(7):
        lmsg(i).wait_send()

    @pl.when(not_last)
    def _():
        @pl.loop(0, ROWS)
        def _(c):
            act_copy(c).wait_send()

    @pl.when(not_first)
    def _():
        @pl.loop(0, ROWS)
        def _(c):
            back_copy(c).wait_send()

    pltpu.make_async_copy(OA, OA, osem.at[0]).wait()
    pltpu.make_async_copy(OB, OB, osem.at[1]).wait()


def finish(acts, grads, down, up, lg, wd, gain, o_acts, o_grads, o_down, o_up, o_gin, o_glat, pad):
    d = lax.axis_index("dp")
    o_acts[...] = acts[...]
    o_grads[...] = grads[...]

    @pl.when(pl.program_id(0) == 0)
    def _():
        o_down[...] = down[...]
        o_up[...] = up[...]
        pad[pl.ds(0, UNIT)] = down[...] * wd[...].astype(F32)
        pad[pl.ds(UNIT, R - UNIT)] = jnp.zeros((R - UNIT, R), F32)
        sums = jnp.sum(pad[...].T, axis=0, keepdims=True)
        first = d * UNIT
        start = pl.multiple_of(jnp.minimum(first // 128 * 128, D - 384), 128)
        window = jnp.broadcast_to(gain[:, pl.ds(start, 384)], (8, 384))
        own = pltpu.roll(window, (384 - (first - start)) % 384, 1)
        o_gin[...] = sums[:, :UNIT] / own[0:1, :UNIT]
        o_glat[...] = pltpu.roll(lg[...], (R - 8 * d) % R, 1)[0:1, :8]


def on_device(
    inflow, entering, arrive_grad, enter_grad, stashed, w_down, w_up, norm_gain, latent_gain
):
    anyspace = pl.BlockSpec(memory_space=pl.ANY)
    vmem = pl.BlockSpec(memory_space=pltpu.VMEM)
    block = pl.BlockSpec((T // 2, D), lambda i: (i, 0))
    rows = (ROWS, T, ROW)
    dma = pltpu.SemaphoreType.DMA
    acts, grads, down, up, lg = pl.pallas_call(
        kernel,
        out_shape=(
            jax.ShapeDtypeStruct((T, D), BF16),
            jax.ShapeDtypeStruct((T, D), BF16),
            jax.ShapeDtypeStruct((UNIT, R), F32),
            jax.ShapeDtypeStruct((UNIT, R), F32),
            jax.ShapeDtypeStruct((8, R), F32),
        ),
        in_specs=[anyspace] * 7 + [vmem] * 2,
        out_specs=(anyspace, anyspace, vmem, vmem, vmem),
        scratch_shapes=[
            pltpu.VMEM((2, 2, 4, 4, UNIT, R), BF16),
            pltpu.VMEM((2, 2, 4, 4, UNIT, R), BF16),
            pltpu.VMEM((2,) + rows, BF16),
            pltpu.VMEM((ROWS, 2 * T, ROW), BF16),
            pltpu.VMEM((ROWS, ROW, 2 * T), BF16),
            pltpu.VMEM((ROWS, 2 * T, ROW), BF16),
            pltpu.VMEM(rows, BF16),
            pltpu.VMEM(rows, BF16),
            pltpu.VMEM(rows, BF16),
            pltpu.VMEM(rows, BF16),
            pltpu.VMEM(rows, BF16),
            pltpu.VMEM(rows, BF16),
            pltpu.VMEM((8, 4, HALF, R), BF16),
            pltpu.VMEM((8, 2, 4, HALF, R), BF16),
            pltpu.VMEM((8, NEAR, R), BF16),
            pltpu.VMEM((8, FAR, R), BF16),
            pltpu.VMEM((4, HALF, R), BF16),
            pltpu.VMEM((8, 2, HALF, R), BF16),
            pltpu.VMEM((2, UNIT, R), BF16),
            pltpu.VMEM((2 * T, R), F32),
            pltpu.VMEM((2 * T, R), F32),
            pltpu.VMEM((2 * T, 1), F32),
            pltpu.VMEM((2 * T, R), BF16),
            pltpu.VMEM((T, R), BF16),
            pltpu.VMEM((2, T, R), F32),
            pltpu.VMEM((2 * T, R), BF16),
            pltpu.VMEM((2, T, 1), F32),
            pltpu.VMEM((2, T, 1), F32),
            pltpu.VMEM((3, 8, R), F32),
            pltpu.VMEM((7, 8, R), F32),
            dma((120,)), dma((120,)),
            dma((4,)), dma((4,)),
            dma((128,)), dma((128,)),
            dma((ROWS,)), dma((ROWS,)),
            dma((ROWS,)), dma((ROWS,)),
            dma((7,)), dma((7,)),
            dma((5,)), dma((2,)),
            pltpu.SemaphoreType.REGULAR,
        ],
        compiler_params=pltpu.CompilerParams(
            collective_id=0, has_side_effects=True, vmem_limit_bytes=60 * 1024 * 1024
        ),
        name="relay",
    )(
        inflow[0], entering[0], arrive_grad[0], enter_grad[0], stashed[0],
        w_down[0], w_up[0].T, norm_gain, latent_gain,
    )
    outs = pl.pallas_call(
        finish,
        out_shape=(
            jax.ShapeDtypeStruct((T, D), BF16),
            jax.ShapeDtypeStruct((T, D), BF16),
            jax.ShapeDtypeStruct((UNIT, R), F32),
            jax.ShapeDtypeStruct((UNIT, R), F32),
            jax.ShapeDtypeStruct((1, UNIT), F32),
            jax.ShapeDtypeStruct((1, 8), F32),
        ),
        grid=(2,),
        in_specs=[block, block] + [vmem] * 5,
        out_specs=(block, block) + (vmem,) * 4,
        scratch_shapes=[pltpu.VMEM((R, R), F32)],
        name="finish",
    )(acts, grads, down, up, lg, w_down[0], norm_gain)
    acts, grads, down, up, gin, glat = outs
    return acts[None], grads[None], down[None], up.T[None], gin, glat


def solution(mesh):
    in_specs = (
        P("section", "dp", None),
        P(None, "dp", None),
        P("section", "dp", None),
        P(None, "dp", None),
        P("section", "dp", None),
        P("section", "dp", None),
        P("section", None, "dp"),
        P("section", None),
        P("section", None),
    )
    out_specs = (
        P("section", "dp", None),
        P("section", "dp", None),
        P("section", "dp", None),
        P("section", None, "dp"),
        P("section", "dp"),
        P("section", "dp"),
    )
    return jax.shard_map(
        on_device, mesh=mesh, in_specs=in_specs, out_specs=out_specs, check_vma=False
    )
```
